256 devices in a mesh: ctx: 32 (over y, z), head: 2 (over x_hi), inst: 4 (over x_lo, core).
Axes of the slice: x: 4 (x_hi: 2, x_lo: 2; x = x_hi * 2 + x_lo), y: 4, z: 8, core: 2. Of those that a mesh axis runs over, the one named last changes fastest.
Arguments:
- queries: bfloat16 [4096, 8, 8, 128], P('ctx', ('head', 'inst')), may hold values from -8 to 8
- cache_kv: bfloat16 [16384, 2, 8, 128], P('ctx', None, ('head', 'inst')), may hold values from -12 to 12
- new_kv: bfloat16 [4096, 2, 8, 128], P('ctx', None, ('head', 'inst')), may hold values from -12 to 12
- cache_lengths: int32 [32], replicated, may hold values from 64 to 512, as said below
- plan: int32 [256, 1], P('ctx'), may hold values from 0 to 3; in each aligned block of 8 rows (0 to 7, 8 to 15, ...) at most 4 rows name the same one
Outputs:
- attended: bfloat16 [4096, 8, 8, 128], P('ctx', ('head', 'inst'))
- migrated: bfloat16 [4, 32, 4, 16, 2, 8, 128], P('inst', 'ctx', 'head')
The draws below stay inside these ranges and needn't reach their ends.
Inputs may be any that keep to these rules, and one draw needn't show every extreme that they name: Shard i's usable slots are its first cache_lengths[i]; some shard is full. `plan`: in the pages of one index of ctx (aligned blocks of 8 rows) no instance is named more than 4 times.
All inputs are finite; a program needn't handle non-finite values.
Results may differ from the reference program's by a relative error of at most 0.006.
Values may be sent and summed in bfloat16 or wider, within the bound.
A program may use at most 64 MiB of HBM per device.

```python
import math
import jax
import jax.numpy as jnp
import numpy as np
from jax import lax

KVH = 8
GROUP = 8
HD = 128
Q_DEV = 128
CACHE_DEV = 512
BLOCK = 16
QTOK = 4096
CACHE = 16384
QBLOCKS = 256
CAP = 4
N_CTX = 32
N_INST = 4


def draw_queries(key, part):
    key = jax.random.fold_in(key, 5)
    shape = (QTOK, KVH, GROUP, HD)
    base = jnp.clip(jax.random.normal(key, shape, jnp.float32), -8.0, 8.0)
    return base.astype(jnp.bfloat16)


def draw_cache_kv(key, part):
    key = jax.random.fold_in(key, 9)
    key_part, value_part = jax.random.split(key)
    shape = (CACHE, KVH, HD)
    key_rows = jnp.clip(2.5 * jax.random.normal(key_part, shape, jnp.float32), -12.0, 12.0)
    value_rows = jnp.clip(2.0 * jax.random.normal(value_part, shape, jnp.float32), -12.0, 12.0)
    return jnp.stack([key_rows, value_rows], axis=1).astype(jnp.bfloat16)


def draw_cache_lengths(key, part):
    key = jax.random.fold_in(key, 17)
    first_key, second_key, third_key = jax.random.split(key, 3)
    base = jax.random.randint(first_key, (N_CTX,), CACHE_DEV // 2, CACHE_DEV + 1)
    halvings = jax.random.randint(second_key, (N_CTX,), 0, 3)
    shrunk = base // jnp.left_shift(jnp.ones((N_CTX,), jnp.int32), halvings)
    fullest = jax.random.randint(third_key, (), 0, N_CTX)
    return jnp.where(jnp.arange(N_CTX) == fullest, CACHE_DEV, shrunk).astype(jnp.int32)


def block_levels(key, shape, pieces, smallest, high):
    def one(dim, parts):
        draws = jax.random.uniform(jax.random.fold_in(jax.random.fold_in(key, 6), dim), (parts,), jnp.float32, smallest / len(pieces), high / len(pieces))
        return jnp.repeat(jnp.exp(draws), shape[dim] // parts).reshape((-1,) + (1,) * (len(shape) - dim - 1))

    loudness = one(*pieces[0])
    for cut in pieces[1:]:
        loudness = loudness * one(*cut)
    return loudness


def shared_out(stream_key, own, number, rows, count, top, limit, skew):
    ranking = jax.random.permutation(stream_key, count)
    crowded, ordinary = shares(count, rows * top, limit, skew, True), shares(count, rows * top, limit, skew, False)
    places = jnp.arange(count)

    def named(tallies, offset_by):
        used = int((tallies > 0).sum())
        fixed = max(1, used // 4)
        passed = fixed + (places - fixed + offset_by * (used - fixed)) % max(1, count - fixed)
        return jnp.zeros((count,), jnp.int32).at[ranking[jnp.where(places < fixed, places, passed)]].set(jnp.asarray(tallies, jnp.int32))

    tallies = jnp.where(number % 4 == 0, named(crowded, number // 4), named(ordinary, number - number // 4 - 1))
    mixed = jax.random.permutation(jax.random.fold_in(own, 3), count)
    giver, receiver = mixed[0:count // 2 * 2:2], mixed[1:count // 2 * 2:2]
    slack = jnp.minimum(tallies[giver] - 1, limit - tallies[receiver]) // 2
    slack = jnp.where((giver == ranking[0]) | (receiver == ranking[0]) | (tallies[receiver] == 0), 0, jnp.maximum(slack, 0))
    passed = jax.random.randint(jax.random.fold_in(own, 4), (count // 2,), 0, 1 << 20) % (slack + 1)
    tallies = tallies.at[giver].add(-passed).at[receiver].add(passed)
    items = jnp.searchsorted(jnp.cumsum(tallies), jnp.arange(rows * top), side="right").astype(jnp.int32)
    table = items.reshape(top, rows).T
    table = table[jax.random.permutation(jax.random.fold_in(own, 1), rows)]
    offset_by = jax.random.randint(jax.random.fold_in(own, 2), (rows, 1), 0, top)
    return jnp.take_along_axis(table, (jnp.arange(top)[None, :] + offset_by) % top, axis=1)


def shares(count, total, bound, skew, full):
    portions = [(1 << 20) // math.isqrt(grade ** skew) + 1 for grade in range(1, count + 1)]
    largest = bound if full else min(bound, max(-(-total // count), total * portions[0] // sum(portions)))
    least = 1 if total - largest >= count - 1 else 0
    holding, rest = [largest] + [least] * (count - 1), total - largest - least * (count - 1)
    while rest > 0:
        candidates = [i for i in range(1, count) if holding[i] < largest] or [i for i in range(1, count) if holding[i] < bound]
        mass, remaining = sum([portions[i] for i in candidates]), rest
        for i in candidates:
            extra = min(bound - holding[i], max(1, remaining * portions[i] // mass), rest)
            holding[i] = holding[i] + extra
            rest = rest - extra
    return np.array(holding)


def noise(own_key, extent, spread, bound, pieces=(), dtype=jnp.bfloat16):
    result = spread * jax.random.normal(own_key, extent, jnp.float32)
    if pieces:
        result = result * block_levels(own_key, extent, pieces, -0.22, 0.18)
    return jnp.clip(result, -bound, bound).astype(dtype)


def setup_inputs(seed: int = 0) -> dict:
    streams_of = jax.random.split(jax.random.key(seed), 6)
    queries = draw_queries(jax.random.fold_in(streams_of[5], 71), 0)
    cache_kv = draw_cache_kv(jax.random.fold_in(streams_of[5], 71), 0)
    new_kv = noise(streams_of[2], (QTOK, 2, KVH, HD), 2.0, 12.0, ((0, 32), (2, 8)))
    cache_lengths = draw_cache_lengths(jax.random.fold_in(streams_of[5], 71), 0)
    plan_keys = jax.random.split(jax.random.fold_in(streams_of[4], 1), QBLOCKS // (Q_DEV // BLOCK))
    plan_turns = jax.random.permutation(jax.random.fold_in(streams_of[4], 3), QBLOCKS // (Q_DEV // BLOCK))
    plan = jax.vmap(lambda own, number: shared_out(jax.random.fold_in(streams_of[4], 2), own, number, Q_DEV // BLOCK, N_INST, 1, CAP, 2))(plan_keys, plan_turns).reshape((QBLOCKS, 1))
    return dict(queries=queries, cache_kv=cache_kv, new_kv=new_kv, cache_lengths=cache_lengths, plan=plan)


masked_score = -1.0e30


def reference(queries, cache_kv, new_kv, cache_lengths, plan):
    score_scale = HD ** -0.5
    cache_rows = jnp.arange(CACHE)
    cache_usable = (cache_rows % CACHE_DEV) < cache_lengths[cache_rows // CACHE_DEV]
    key_tokens = jnp.arange(QTOK)
    query_heads = jnp.transpose(queries, (1, 0, 2, 3)).reshape(KVH, N_CTX, Q_DEV * GROUP, HD)
    query_pos = jnp.repeat(jnp.arange(QTOK), GROUP).reshape(N_CTX, Q_DEV * GROUP)
    cache_keys = jnp.transpose(cache_kv[:, 0], (1, 0, 2))
    cache_vals = jnp.transpose(cache_kv[:, 1], (1, 0, 2))
    stretch_keys = jnp.transpose(new_kv[:, 0], (1, 0, 2))
    stretch_vals = jnp.transpose(new_kv[:, 1], (1, 0, 2))

    def one_head(head_args):
        query_head, head_ckeys, head_cvals, head_nkeys, head_nvals = head_args

        def one_block(block_args):
            query_block, block_pos = block_args
            cache_scores = jnp.dot(query_block, head_ckeys.T, preferred_element_type=jnp.float32) * score_scale
            stretch_scores = jnp.dot(query_block, head_nkeys.T, preferred_element_type=jnp.float32) * score_scale
            stretch_usable = key_tokens[None, :] <= block_pos[:, None]
            row_max = jnp.maximum(
                jnp.max(jnp.where(cache_usable[None, :], cache_scores, masked_score), axis=1),
                jnp.max(jnp.where(stretch_usable, stretch_scores, masked_score), axis=1))
            cache_weights = jnp.where(cache_usable[None, :], jnp.exp(cache_scores - row_max[:, None]), 0.0)
            stretch_weights = jnp.where(stretch_usable, jnp.exp(stretch_scores - row_max[:, None]), 0.0)
            weight_sum = jnp.sum(cache_weights, axis=1) + jnp.sum(stretch_weights, axis=1)
            mixed_rows = jnp.dot(cache_weights.astype(jnp.bfloat16), head_cvals, preferred_element_type=jnp.float32)
            mixed_rows = mixed_rows + jnp.dot(stretch_weights.astype(jnp.bfloat16), head_nvals, preferred_element_type=jnp.float32)
            return (mixed_rows / weight_sum[:, None]).astype(jnp.bfloat16)

        return lax.map(one_block, (query_head, query_pos))

    attended = lax.map(one_head, (query_heads, cache_keys, cache_vals, stretch_keys, stretch_vals))
    attended = jnp.transpose(attended.reshape(KVH, QTOK, GROUP, HD), (1, 0, 2, 3))

    dev_blocks = Q_DEV // BLOCK
    destination = plan[:, 0].reshape(N_CTX, dev_blocks)
    block_order = jnp.arange(dev_blocks)
    earlier = (block_order[:, None] < block_order[None, :])[None, :, :] & (destination[:, :, None] == destination[:, None, :])
    slot_index = jnp.sum(earlier.astype(jnp.int32), axis=1)
    target = destination * CAP + slot_index
    select = (jnp.arange(N_INST * CAP)[None, :, None] == target[:, None, :]).astype(jnp.float32)
    page_rows = new_kv.reshape(N_CTX, dev_blocks, BLOCK * 2 * KVH * HD).astype(jnp.float32)
    arrived = jnp.einsum('nsb,nbf->nsf', select, page_rows)
    arrived = arrived.reshape(N_CTX, N_INST, CAP, BLOCK, 2, KVH, HD)
    migrated = jnp.transpose(arrived, (1, 0, 2, 3, 4, 5, 6)).astype(jnp.bfloat16)
    return attended, migrated
```

```python
import functools
import math

import jax
import jax.numpy as jnp
from jax import lax
from jax.experimental import pallas as pl
from jax.experimental.pallas import tpu as pltpu
from jax.sharding import PartitionSpec as P

MESH = pl.DeviceIdType.MESH
NY, NZ = 4, 8
NH, NI = 2, 4
HD = 128
GROUP = 8
TOK = 128
ROWS = TOK * GROUP
CACHE = 512
HALF = CACHE // 2
STEP = 4 * HALF
PAIR = 2 * TOK
TILE = 512
NQT = NY * ROWS // TILE
BLOCK = 16
PAGES = TOK // BLOCK
CAP = PAGES // 2
SCALE = HD ** -0.5 * math.log2(math.e)
LOWEST = -1.0e30
NT = (((1,), (1,)), ((), ()))

HALVES = (
    (0, 0), (0, 1), (1, 0), (-1, 0),
    (1, 1), (-1, 1), (2, 0), (-2, 0),
    (2, 1), (-2, 1), (3, 0), (-3, 0),
    (3, 1), (-3, 1), (4, 0), (4, 1),
)
TO_NEXT = {0: 3, 1: 5, 3: 7, 5: 9, 7: 11, 9: 13, 11: 14}
TO_PREV = {0: 2, 1: 4, 2: 6, 4: 8, 6: 10, 8: 12, 12: 15}
OFFSETS = (0, 1, 3, 2)


def kernel(lens, plan, q_in, cache_in, fresh_in, out, moved,
           kv, st, qs, acc, top, sbuf, wide, packed, osend, lsend, oget, lget,
           kv_s, kv_r, st_s, st_r, sh_s, sh_r, q_s, q_r, o_s, o_r, l_s, l_r, mg_s, mg_r, own_s):
    ctx = lax.axis_index("ctx")
    head = lax.axis_index("head")
    inst = lax.axis_index("inst")
    y, z = ctx // NZ, ctx % NZ
    me = head * NI + inst

    def at_z(d):
        return (y * NZ + (z + d + NZ) % NZ, head, inst)

    def at_y(d):
        return (((y + d + NY) % NY) * NZ + z, head, inst)

    def at_head(h):
        return (ctx, h // NI, h % NI)

    barrier = pltpu.get_barrier_semaphore()
    peers = [at_z(1), at_z(-1), at_y(1), at_y(2), at_y(3)]
    peers += [at_head((me + d) % (NH * NI)) for d in range(1, NH * NI)]
    for peer in peers:
        pl.semaphore_signal(barrier, inc=1, device_id=peer, device_id_type=MESH)

    length = lens[ctx]
    wide[...] = cache_in[...].astype(jnp.float32)
    slot_no = lax.broadcasted_iota(jnp.int32, (CACHE, HD), 0)
    keys = wide[pl.ds(0, CACHE, stride=2), :]
    values = wide[pl.ds(1, CACHE, stride=2), :]
    keys = jnp.where(slot_no < length, keys, jnp.broadcast_to(keys[0:1, :], (CACHE, HD)))
    values = jnp.where(slot_no < length, values, 0.0)
    kv[pl.ds(0, CACHE), 0:HD] = keys.astype(jnp.bfloat16)
    kv[pl.ds(0, CACHE), HD:2 * HD] = values.astype(jnp.bfloat16)
    fresh = fresh_in[...].astype(jnp.float32)
    wide[pl.ds(0, 2 * TOK), :] = fresh
    mine = st.at[pl.ds(NZ * TOK, TOK)]
    mine[:, 0:HD] = wide[pl.ds(0, TOK, stride=2), :].astype(jnp.bfloat16)
    mine[:, HD:2 * HD] = wide[pl.ds(1, TOK, stride=2), :].astype(jnp.bfloat16)
    qs[pl.ds(0, ROWS), :] = q_in[...]

    def kv_copy(src, forward):
        dst = (TO_NEXT if forward else TO_PREV)[src]
        return pltpu.make_async_remote_copy(
            src_ref=kv.at[pl.ds(src * HALF, HALF), pl.ds(0, 2 * HD)],
            dst_ref=kv.at[pl.ds(dst * HALF, HALF), pl.ds(0, 2 * HD)],
            send_sem=kv_s.at[dst],
            recv_sem=kv_r.at[dst],
            device_id=at_z(1 if forward else -1),
            device_id_type=MESH,
        )

    def kv_arrived(dst):
        forward = dst in TO_NEXT.values()
        src = {b: a for a, b in (TO_NEXT if forward else TO_PREV).items()}[dst]
        kv_copy(src, forward).wait_recv()

    def kv_sent(dst):
        forward = dst in TO_NEXT.values()
        src = {b: a for a, b in (TO_NEXT if forward else TO_PREV).items()}[dst]
        kv_copy(src, forward).wait_send()

    def q_copy(n):
        half = (0, 1, 0, 1, 0, 1)[n]
        src = (0, 0, 0, 0, 2, 1)[n]
        dst = (2, 2, 1, 1, 3, 3)[n]
        to = (1, 1, -1, -1, 1, -1)[n]
        return pltpu.make_async_remote_copy(
            src_ref=qs.at[pl.ds(src * ROWS + half * TILE, TILE)],
            dst_ref=qs.at[pl.ds(dst * ROWS + half * TILE, TILE)],
            send_sem=q_s.at[n],
            recv_sem=q_r.at[n],
            device_id=at_y(to),
            device_id_type=MESH,
        )

    def place(zz):
        return ((zz % NY) * 2 + zz // NY) * TOK

    def shift_copy():
        return pltpu.make_async_remote_copy(
            src_ref=st.at[pl.ds(NZ * TOK, TOK), pl.ds(0, 2 * HD)],
            dst_ref=st.at[pl.ds(pl.multiple_of(place(z), TOK), TOK), pl.ds(0, 2 * HD)],
            send_sem=sh_s,
            recv_sem=sh_r,
            device_id=(((y - z + NZ) % NY) * NZ + z, head, inst),
            device_id_type=MESH,
        )

    def stay_copy():
        return pltpu.make_async_copy(
            st.at[pl.ds(NZ * TOK, TOK), pl.ds(0, 2 * HD)],
            st.at[pl.ds(pl.multiple_of(place(z), TOK), TOK), pl.ds(0, 2 * HD)],
            sh_r,
        )

    def st_rows(zz, hop, forward):
        start = place((zz + NZ) % NZ)
        if hop < 4:
            return pl.ds(pl.multiple_of(start, TOK), TOK)
        half = TOK // 2
        return pl.ds(pl.multiple_of(start + (0 if forward else half), half), half)

    def st_copy(hop, forward):
        sign = 1 if forward else -1
        rows = st_rows(z - sign * (hop - 1), hop, forward)
        return pltpu.make_async_remote_copy(
            src_ref=st.at[rows, pl.ds(0, 2 * HD)],
            dst_ref=st.at[rows, pl.ds(0, 2 * HD)],
            send_sem=st_s.at[hop - 1, int(forward)],
            recv_sem=st_r.at[hop - 1, int(forward)],
            device_id=at_z(sign),
            device_id_type=MESH,
        )

    def st_arrived(hop, forward):
        sign = 1 if forward else -1
        rows = st_rows(z - sign * hop, hop, forward)
        pltpu.make_async_remote_copy(
            src_ref=st.at[rows, pl.ds(0, 2 * HD)],
            dst_ref=st.at[rows, pl.ds(0, 2 * HD)],
            send_sem=st_s.at[hop - 1, int(forward)],
            recv_sem=st_r.at[hop - 1, int(forward)],
            device_id=at_z(sign),
            device_id_type=MESH,
        ).wait_recv()

    def page_copy(d, dst):
        to = (me + d) % (NH * NI)
        return pltpu.make_async_remote_copy(
            src_ref=packed.at[(to % NI) * NH + to // NI],
            dst_ref=moved.at[dst],
            send_sem=mg_s.at[d],
            recv_sem=mg_r.at[d],
            device_id=at_head(to),
            device_id_type=MESH,
        )

    def own_pages():
        return pltpu.make_async_copy(packed.at[inst * NH + head], moved.at[me], own_s)

    def o_copy(a):
        return pltpu.make_async_remote_copy(
            src_ref=osend.at[a - 1],
            dst_ref=oget.at[a - 1],
            send_sem=o_s.at[a - 1],
            recv_sem=o_r.at[a - 1],
            device_id=at_y(OFFSETS[a]),
            device_id_type=MESH,
        )

    def l_copy(a):
        return pltpu.make_async_remote_copy(
            src_ref=lsend.at[a - 1],
            dst_ref=lget.at[a - 1],
            send_sem=l_s.at[a - 1],
            recv_sem=l_r.at[a - 1],
            device_id=at_y(OFFSETS[a]),
            device_id_type=MESH,
        )

    pl.semaphore_wait(barrier, len(peers))

    for half in (0, 1):
        kv_copy(half, True).start()
        kv_copy(half, False).start()
        q_copy(half).start()
        q_copy(2 + half).start()

    @pl.when(z % NY != 0)
    def _():
        shift_copy().start()

    @pl.when(z % NY == 0)
    def _():
        stay_copy().start()

    targets = []
    for b in range(PAGES):
        earlier = jnp.int32(0)
        for a in range(b):
            earlier = earlier + (plan[a] == plan[b]).astype(jnp.int32)
        targets.append(plan[b] * CAP + earlier)
    for t in range(NI * CAP):
        page = jnp.zeros((2 * BLOCK, HD), jnp.float32)
        for b in range(PAGES):
            page = page + fresh[2 * BLOCK * b:2 * BLOCK * (b + 1), :] * (targets[b] == t).astype(jnp.float32)
        packed[t // 2, pl.ds((t % 2) * 2 * BLOCK, 2 * BLOCK), :] = page.astype(jnp.bfloat16)
    for d in range(1, NH * NI):
        page_copy(d, me).start()
    own_pages().start()

    row_no = lax.broadcasted_iota(jnp.int32, (HALF, HD), 0)
    for n, (d, half) in enumerate(HALVES):
        filled = lens[y * NZ + (z + d + NZ) % NZ]
        kv[pl.ds(n * HALF, HALF), 2 * HD:3 * HD] = jnp.where(
            row_no + half * HALF < filled, 1.0, 0.0
        ).astype(jnp.bfloat16)
    st[pl.ds(0, NZ * TOK), 2 * HD:3 * HD] = jnp.ones((NZ * TOK, HD), jnp.bfloat16)

    def empty(n, carry):
        rows = pl.ds(pl.multiple_of(n * TILE, TILE), TILE)
        acc[rows, :] = jnp.zeros((TILE, 2 * HD), jnp.float32)
        top[rows, :] = jnp.full((TILE, HD), LOWEST, jnp.float32)
        return carry

    lax.fori_loop(0, NQT, empty, 0)

    def add(rows, scores, vals):
        before = top[rows, :]
        peak = jnp.maximum(before, jnp.max(scores, axis=1, keepdims=True) * SCALE)
        factor = jnp.exp2(before - peak)
        weights = jnp.exp2(scores * SCALE - peak[:, :1]).astype(jnp.bfloat16)
        part = jnp.dot(weights, vals, preferred_element_type=jnp.float32)
        acc[rows, :] = acc[rows, :] * jnp.concatenate([factor, factor], axis=1) + part
        top[rows, :] = peak

    def q_rows(i):
        return pl.ds(pl.multiple_of((i % NQT) * TILE, TILE), TILE)

    def kv_rows(i):
        return pl.ds(pl.multiple_of((i // NQT) * STEP, STEP), STEP)

    def score(i, slot):
        sbuf[slot] = lax.dot_general(
            qs[q_rows(i), :], kv[kv_rows(i), 0:HD], NT, preferred_element_type=jnp.float32
        )

    def weigh(i, slot):
        add(q_rows(i), sbuf[slot], kv[kv_rows(i), HD:3 * HD])

    def pass_on(dst):
        kv_arrived(dst)
        if dst in TO_NEXT and dst not in TO_PREV:
            kv_copy(dst, True).start()
        elif dst in TO_PREV:
            kv_copy(dst, False).start()

    def at_0():
        q_copy(2).wait_recv()

    def at_1():
        q_copy(3).wait_recv()
        q_copy(5).start()
        q_copy(0).wait_recv()
        q_copy(4).start()
        pass_on(4)
        pass_on(5)

    def at_2():
        q_copy(1).wait_recv()
        q_copy(4).wait_recv()

        @pl.when(z % NY != 0)
        def _():
            shift_copy().wait_recv()

        @pl.when(z % NY == 0)
        def _():
            stay_copy().wait()

        for forward in (True, False):
            st_copy(1, forward).start()

    def at_3():
        q_copy(5).wait_recv()
        pass_on(6)
        pass_on(7)

    def at_4():
        pass_on(8)
        pass_on(9)

    def next_stretch(hop):
        for forward in (True, False):
            st_arrived(hop, forward)
            st_copy(hop + 1, forward).start()

    def at_6():
        pass_on(10)
        pass_on(11)

    def at_8():
        pass_on(12)
        pass_on(13)

    def at_11():
        pass_on(14)
        pass_on(15)

    events = {
        0: at_0, 1: at_1, 2: at_2, 3: at_3, 4: at_4, 5: lambda: next_stretch(1), 6: at_6,
        7: lambda: next_stretch(2), 8: at_8, 9: lambda: next_stretch(3), 11: at_11,
    }

    pass_on(2)
    pass_on(3)
    score(0, 0)
    last = 4 * NQT // 2 - 1

    def two_tiles(n, carry):
        for when, event in events.items():
            pl.when(n == when)(event)
        for u in (0, 1):
            i = 2 * n + u
            score(i + 1, 1 - u)
            weigh(i, u)
        return carry

    lax.fori_loop(0, last, two_tiles, 0)
    score(2 * last + 1, 1)
    weigh(2 * last, 0)
    weigh(2 * last + 1, 1)

    for forward in (True, False):
        st_arrived(4, forward)

    eye = (
        lax.broadcasted_iota(jnp.int32, (HD, HD), 0) == lax.broadcasted_iota(jnp.int32, (HD, HD), 1)
    ).astype(jnp.float32)

    def stretch(a, row):
        starts = [pl.multiple_of(((j - y + NY) % NY) * PAIR, PAIR) for j in range(row + 1)]
        k_here = jnp.concatenate([st[pl.ds(s, PAIR), 0:HD] for s in starts], axis=0)
        v_here = jnp.concatenate([st[pl.ds(s, PAIR), HD:3 * HD] for s in starts], axis=0)
        column = lax.broadcasted_iota(jnp.int32, (TILE, PAIR), 1)
        token = lax.broadcasted_iota(jnp.int32, (TILE, PAIR), 0) // GROUP
        first = ((row - y + NY) % NY) * TOK
        key_pos = first + column + jnp.where(column >= TOK, NY * TOK - TOK, 0)
        tiles = [pl.ds(pl.multiple_of(a * ROWS + n * TILE, TILE), TILE) for n in range(ROWS // TILE)]
        scored = []
        for n, rows in enumerate(tiles):
            s = lax.dot_general(qs[rows, :], k_here, NT, preferred_element_type=jnp.float32)
            usable = key_pos <= z * TOK + n * (TILE // GROUP) + token
            own = jnp.where(usable, s[:, row * PAIR:], LOWEST)
            scored.append(own if row == 0 else jnp.concatenate([s[:, :row * PAIR], own], axis=1))
        for rows, s in zip(tiles, scored):
            add(rows, s, v_here)

    def finish(rows):
        part = acc[rows, :]
        total = part[:, HD:]
        result = part[:, :HD] / total
        level = top[rows, :] + jnp.log2(total)
        return result, level

    def stretch_of(a):
        offset = jnp.where(a == 0, 0, jnp.where(a == 1, 1, jnp.where(a == 2, 3, 2)))
        mine_row = (y + offset) % NY
        for row in range(NY):
            pl.when(mine_row == row)(functools.partial(stretch, a, row))

    def hand_back(a):
        stretch_of(a)
        for n in range(ROWS // HD):
            result, level = finish(pl.ds(pl.multiple_of(a * ROWS + n * HD, HD), HD))
            osend[a - 1, pl.ds(n * HD, HD), :] = result.astype(jnp.bfloat16)
            lsend[a - 1, pl.ds(n, 1), :] = jnp.sum(level * eye, axis=0, keepdims=True)

    for a in (3, 1, 2):
        hand_back(a)
        o_copy(a).start()
        l_copy(a).start()
    stretch_of(0)

    levels = []
    for n in range(ROWS // HD):
        result, level = finish(pl.ds(n * HD, HD))
        acc[pl.ds(n * HD, HD), 0:HD] = result
        levels.append(jnp.sum(level * eye, axis=0, keepdims=True))
    levels = [jnp.concatenate(levels, axis=0)]
    for a in (3, 1, 2):
        l_copy(a).wait_recv()
        levels.append(lget[a - 1])
    peak = functools.reduce(jnp.maximum, levels)
    shares = [jnp.exp2(level - peak) for level in levels]
    total = functools.reduce(jnp.add, shares)
    shares = [share / total for share in shares]
    for a in (3, 1, 2):
        o_copy(a).wait_recv()
    ones = jnp.ones((2 * HD, HD), jnp.bfloat16)
    for n in range(ROWS // HD):
        rows = pl.ds(n * HD, HD)
        result = jnp.zeros((HD, HD), jnp.float32)
        for share, part in zip(shares, (acc[rows, 0:HD], oget[2, rows, :], oget[0, rows, :], oget[1, rows, :])):
            diagonal = jnp.broadcast_to(share[n:n + 1, :], (HD, HD)) * eye
            high = diagonal.astype(jnp.bfloat16)
            low = (diagonal - high.astype(jnp.float32)).astype(jnp.bfloat16)
            spread = jnp.dot(jnp.concatenate([high, low], axis=1), ones, preferred_element_type=jnp.float32)
            result = result + spread * part.astype(jnp.float32)
        out[rows, :] = result.astype(jnp.bfloat16)

    for dst in range(2, 16):
        kv_sent(dst)
    for n in range(6):
        q_copy(n).wait_send()
    for hop in (1, 2, 3, 4):
        for forward in (True, False):
            st_copy(hop, forward).wait_send()

    @pl.when(z % NY != 0)
    def _():
        shift_copy().wait_send()

    for a in (1, 2, 3):
        o_copy(a).wait_send()
        l_copy(a).wait_send()
    for d in range(1, NH * NI):
        page_copy(d, me).wait_send()
        page_copy(d, (me - d + NH * NI) % (NH * NI)).wait_recv()
    own_pages().wait()


def body(queries, cache_kv, new_kv, cache_lengths, plan):
    smem = pl.BlockSpec(memory_space=pltpu.SMEM)
    vmem = pl.BlockSpec(memory_space=pltpu.VMEM)
    heads = NH * NI
    out, moved = pl.pallas_call(
        kernel,
        out_shape=(
            jax.ShapeDtypeStruct((ROWS, HD), jnp.bfloat16),
            jax.ShapeDtypeStruct((heads, 4 * BLOCK, HD), jnp.bfloat16),
        ),
        in_specs=[smem, smem, vmem, vmem, vmem],
        out_specs=(vmem, pl.BlockSpec(memory_space=pl.ANY)),
        scratch_shapes=[
            pltpu.VMEM((16 * HALF, 3 * HD), jnp.bfloat16),
            pltpu.VMEM(((NZ + 1) * TOK, 3 * HD), jnp.bfloat16),
            pltpu.VMEM((NY * ROWS, HD), jnp.bfloat16),
            pltpu.VMEM((NY * ROWS, 2 * HD), jnp.float32),
            pltpu.VMEM((NY * ROWS, HD), jnp.float32),
            pltpu.VMEM((2, TILE, STEP), jnp.float32),
            pltpu.VMEM((2 * CACHE, HD), jnp.float32),
            pltpu.VMEM((heads, 4 * BLOCK, HD), jnp.bfloat16),
            pltpu.VMEM((3, ROWS, HD), jnp.bfloat16),
            pltpu.VMEM((3, ROWS // HD, HD), jnp.float32),
            pltpu.VMEM((3, ROWS, HD), jnp.bfloat16),
            pltpu.VMEM((3, ROWS // HD, HD), jnp.float32),
            pltpu.SemaphoreType.DMA((16,)),
            pltpu.SemaphoreType.DMA((16,)),
            pltpu.SemaphoreType.DMA((4, 2)),
            pltpu.SemaphoreType.DMA((4, 2)),
            pltpu.SemaphoreType.DMA,
            pltpu.SemaphoreType.DMA,
            pltpu.SemaphoreType.DMA((6,)),
            pltpu.SemaphoreType.DMA((6,)),
            pltpu.SemaphoreType.DMA((3,)),
            pltpu.SemaphoreType.DMA((3,)),
            pltpu.SemaphoreType.DMA((3,)),
            pltpu.SemaphoreType.DMA((3,)),
            pltpu.SemaphoreType.DMA((heads,)),
            pltpu.SemaphoreType.DMA((heads,)),
            pltpu.SemaphoreType.DMA,
        ],
        compiler_params=pltpu.CompilerParams(
            collective_id=0, has_side_effects=True, vmem_limit_bytes=48 * 2 ** 20
        ),
        name="stretch_attention",
    )(
        cache_lengths,
        plan.reshape(PAGES),
        queries.reshape(ROWS, HD),
        cache_kv.reshape(2 * CACHE, HD),
        new_kv.reshape(2 * TOK, HD),
    )
    attended = out.reshape(TOK, 1, GROUP, HD)
    moved = moved.reshape(heads, 2, BLOCK, 2, HD)
    migrated = jnp.transpose(moved, (1, 2, 3, 0, 4)).reshape(1, 1, 2, BLOCK, 2, heads, HD)
    return attended, migrated


def solution(mesh):
    return jax.shard_map(
        body,
        mesh=mesh,
        in_specs=(
            P("ctx", ("head", "inst"), None, None),
            P("ctx", None, ("head", "inst"), None),
            P("ctx", None, ("head", "inst"), None),
            P(),
            P("ctx", None),
        ),
        out_specs=(
            P("ctx", ("head", "inst"), None, None),
            P("inst", "ctx", "head", None, None, None, None),
        ),
        check_vma=False,
    )
```

```python
import functools
import math

import jax
import jax.numpy as jnp
from jax import lax
from jax.experimental import pallas as pl
from jax.experimental.pallas import tpu as pltpu
from jax.sharding import PartitionSpec as P

MESH = pl.DeviceIdType.MESH
NY, NZ = 4, 8
NH, NI = 2, 4
HEADS = NH * NI
HD = 128
GROUP = 8
TOK = 128
ROWS = TOK * GROUP
CACHE = 512
PIECE = 128
OWN = CACHE // PIECE
MSGS = 14
PIECES = OWN + 2 * MSGS
PER_STEP = 8
STEP = PER_STEP * PIECE
TILE = 512
BLOCK = 16
PAGES = TOK // BLOCK
CAP = PAGES // 2
SUMS = 16
SCALE = HD ** -0.5 * math.log2(math.e)
LOWEST = -1.0e30
NT = (((1,), (1,)), ((), ()))
OFFSETS = (0, 1, 3, 2)


def piece_of(m, forward):
    return OWN + 2 * m + (0 if forward else 1)


def shard_of(m, forward):
    if m < 12:
        hop, quarter = 1 + m // OWN, m % OWN
    else:
        hop, quarter = 4, (m - 12 if forward else m - 10)
    return (-hop if forward else hop), quarter


def next_message(m, forward):
    if m < 8:
        return m + 4
    if forward and m in (8, 9):
        return m + 4
    if not forward and m in (10, 11):
        return m + 2
    return None


def kernel(lens, plan, q_in, cache_in, fresh_in, out, moved,
           kv, st, live, qs, acc, top, sbuf, raw, fraw, wide, packed, osend, lsend, oget, lget,
           in_s, kv_s, kv_r, st_s, st_r, sh_s, sh_r, q_s, q_r, o_s, o_r, l_s, l_r, mg_s, mg_r, own_s):
    ctx = lax.axis_index("ctx")
    head = lax.axis_index("head")
    inst = lax.axis_index("inst")
    y, z = ctx // NZ, ctx % NZ
    me = head * NI + inst

    def at_z(d):
        return (y * NZ + (z + d + NZ) % NZ, head, inst)

    def at_y(d):
        return (((y + d + NY) % NY) * NZ + z, head, inst)

    def at_head(h):
        return (ctx, h // NI, h % NI)

    loads = [
        pltpu.make_async_copy(cache_in.at[pl.ds(n * 2 * PIECE, 2 * PIECE)], raw.at[n], in_s.at[n])
        for n in range(OWN)
    ]
    loads.append(pltpu.make_async_copy(fresh_in, fraw, in_s.at[OWN]))
    loads.append(pltpu.make_async_copy(q_in, qs.at[pl.ds(0, ROWS)], in_s.at[OWN + 1]))
    for load in loads:
        load.start()

    barrier = pltpu.get_barrier_semaphore()
    peers = [at_z(1), at_z(-1), at_y(1), at_y(2), at_y(3)]
    peers += [at_head((me + d) % HEADS) for d in range(1, HEADS)]
    for peer in peers:
        pl.semaphore_signal(barrier, inc=1, device_id=peer, device_id_type=MESH)

    def kv_copy(m, forward):
        if m < OWN:
            src = m
        else:
            before = [b for b in range(MSGS) if next_message(b, forward) == m]
            src = piece_of(before[0], forward)
        dst = piece_of(m, forward)
        return pltpu.make_async_remote_copy(
            src_ref=kv.at[src],
            dst_ref=kv.at[dst],
            send_sem=kv_s.at[dst],
            recv_sem=kv_r.at[dst],
            device_id=at_z(1 if forward else -1),
            device_id_type=MESH,
        )

    def pass_on(m):
        for forward in (True, False):
            kv_copy(m, forward).wait_recv()
            later = next_message(m, forward)
            if later is not None:
                kv_copy(later, forward).start()

    def q_copy(n):
        half = (0, 1, 0, 1, 0, 1)[n]
        src = (0, 0, 0, 0, 2, 1)[n]
        dst = (2, 2, 1, 1, 3, 3)[n]
        to = (1, 1, -1, -1, 1, -1)[n]
        if n < 4:
            src_ref = q_in.at[pl.ds(half * TILE, TILE)]
        else:
            src_ref = qs.at[pl.ds(src * ROWS + half * TILE, TILE)]
        return pltpu.make_async_remote_copy(
            src_ref=src_ref,
            dst_ref=qs.at[pl.ds(dst * ROWS + half * TILE, TILE)],
            send_sem=q_s.at[n],
            recv_sem=q_r.at[n],
            device_id=at_y(to),
            device_id_type=MESH,
        )

    def place(zz):
        zz = (zz + NZ) % NZ
        return (zz % NY) * 2 + zz // NY

    def shift_copy():
        return pltpu.make_async_remote_copy(
            src_ref=st.at[NZ],
            dst_ref=st.at[place(z)],
            send_sem=sh_s,
            recv_sem=sh_r,
            device_id=(((y - z + NZ) % NY) * NZ + z, head, inst),
            device_id_type=MESH,
        )

    def stay_copy():
        return pltpu.make_async_copy(st.at[NZ], st.at[place(z)], sh_r)

    def st_ref(zz, hop, forward):
        if hop < 4:
            return st.at[place(zz)]
        return st.at[place(zz), pl.ds(0 if forward else TOK, TOK)]

    def st_copy(hop, forward, sending):
        sign = 1 if forward else -1
        ref = st_ref(z - sign * (hop - 1 if sending else hop), hop, forward)
        return pltpu.make_async_remote_copy(
            src_ref=ref,
            dst_ref=ref,
            send_sem=st_s.at[hop - 1, int(forward)],
            recv_sem=st_r.at[hop - 1, int(forward)],
            device_id=at_z(sign),
            device_id_type=MESH,
        )

    def next_stretch(hop):
        for forward in (True, False):
            st_copy(hop, forward, False).wait_recv()
            if hop < 4:
                st_copy(hop + 1, forward, True).start()

    def page_copy(d, dst):
        to = (me + d) % HEADS
        return pltpu.make_async_remote_copy(
            src_ref=packed.at[(to % NI) * NH + to // NI],
            dst_ref=moved.at[dst],
            send_sem=mg_s.at[d],
            recv_sem=mg_r.at[d],
            device_id=at_head(to),
            device_id_type=MESH,
        )

    def own_pages():
        return pltpu.make_async_copy(packed.at[inst * NH + head], moved.at[me], own_s)

    def o_copies(n):
        to = at_y((1, -1, 1, 1, -1, -1)[n])
        return (
            pltpu.make_async_remote_copy(
                src_ref=osend.at[n], dst_ref=oget.at[n], send_sem=o_s.at[n], recv_sem=o_r.at[n],
                device_id=to, device_id_type=MESH,
            ),
            pltpu.make_async_remote_copy(
                src_ref=lsend.at[n], dst_ref=lget.at[n], send_sem=l_s.at[n], recv_sem=l_r.at[n],
                device_id=to, device_id_type=MESH,
            ),
        )

    length = lens[ctx]

    def split(n):
        return wide[n, pl.ds(0, PIECE, stride=2), :], wide[n, pl.ds(1, PIECE, stride=2), :]

    def own_piece(n, first):
        loads[n].wait()
        wide[n] = raw[n].astype(jnp.float32)
        keys, values = split(n)
        first = keys[0:1, :] if n == 0 else first
        usable = lax.broadcasted_iota(jnp.int32, (PIECE, HD), 0) + n * PIECE < length
        kv[n, pl.ds(0, PIECE), :] = jnp.where(usable, keys, jnp.broadcast_to(first, (PIECE, HD))).astype(jnp.bfloat16)
        kv[n, pl.ds(PIECE, HD), :] = jnp.where(usable, values, 0.0).T.astype(jnp.bfloat16)
        return first

    first = own_piece(0, None)
    pl.semaphore_wait(barrier, len(peers))
    for forward in (True, False):
        kv_copy(0, forward).start()
    q_copy(0).start()
    q_copy(2).start()
    for n in range(1, OWN):
        own_piece(n, first)
        for forward in (True, False):
            kv_copy(n, forward).start()

    loads[OWN].wait()
    fresh = fraw[...].astype(jnp.float32)
    wide[OWN] = fresh
    keys, values = split(OWN)
    st[NZ, pl.ds(0, TOK), :] = keys.astype(jnp.bfloat16)
    st[NZ, pl.ds(TOK, HD), :] = values.T.astype(jnp.bfloat16)

    @pl.when(z % NY != 0)
    def _():
        shift_copy().start()

    @pl.when(z % NY == 0)
    def _():
        stay_copy().start()

    q_copy(1).start()
    q_copy(3).start()

    def empty(n, carry):
        acc[:, pl.ds(pl.multiple_of(n * TILE, TILE), TILE)] = jnp.zeros((HD + SUMS, TILE), jnp.float32)
        return carry

    lax.fori_loop(0, NY * ROWS // TILE, empty, 0)
    top[...] = jnp.full((1, NY * ROWS), LOWEST, jnp.float32)
    origin = {n: (0, n) for n in range(OWN)}
    for m in range(MSGS):
        for forward in (True, False):
            origin[piece_of(m, forward)] = shard_of(m, forward)
    lane = lax.broadcasted_iota(jnp.int32, (SUMS, PIECE), 1)
    for n in range(PIECES):
        d, quarter = origin[n]
        filled = lens[y * NZ + (z + d + NZ) % NZ]
        live[:, pl.ds(n * PIECE, PIECE)] = jnp.where(lane + quarter * PIECE < filled, 1.0, 0.0).astype(jnp.bfloat16)

    targets = []
    for b in range(PAGES):
        earlier = jnp.int32(0)
        for a in range(b):
            earlier = earlier + (plan[a] == plan[b]).astype(jnp.int32)
        targets.append(plan[b] * CAP + earlier)
    for t in range(NI * CAP):
        page = jnp.zeros((2 * BLOCK, HD), jnp.float32)
        for b in range(PAGES):
            page = page + fresh[2 * BLOCK * b:2 * BLOCK * (b + 1), :] * (targets[b] == t).astype(jnp.float32)
        packed[t // 2, pl.ds((t % 2) * 2 * BLOCK, 2 * BLOCK), :] = page.astype(jnp.bfloat16)
    for d in range(1, HEADS):
        page_copy(d, me).start()
    own_pages().start()

    def columns(a, half):
        return pl.ds(pl.multiple_of(a * ROWS + half * TILE, TILE), TILE)

    def add(cols, scores, vals):
        before = top[:, cols]
        peak = jnp.maximum(before, jnp.max(scores, axis=0, keepdims=True) * SCALE)
        weights = jnp.exp2(scores * SCALE - peak).astype(jnp.bfloat16)
        part = jnp.dot(vals, weights, preferred_element_type=jnp.float32)
        acc[:, cols] = acc[:, cols] * jnp.exp2(before - peak) + part
        top[:, cols] = peak

    def score(a, half, step, slot):
        keys = kv[pl.ds(step * PER_STEP, PER_STEP), pl.ds(0, PIECE), :].reshape(STEP, HD)
        sbuf[slot] = lax.dot_general(keys, qs[columns(a, half), :], NT, preferred_element_type=jnp.float32)

    def weigh(a, half, step, slot):
        vals = jnp.concatenate([kv[step * PER_STEP + n, pl.ds(PIECE, HD), :] for n in range(PER_STEP)], axis=1)
        sums = live[:, pl.ds(pl.multiple_of(step * STEP, STEP), STEP)]
        add(columns(a, half), sbuf[slot], jnp.concatenate([vals, sums], axis=0))

    def turn(n):
        return jnp.where(n < 4, n, (n + 1) % 4), n // 4

    def event_0():
        q_copy(2).wait_recv()
        pass_on(2)

    def event_1():
        q_copy(3).wait_recv()
        q_copy(5).start()
        q_copy(0).wait_recv()
        q_copy(4).start()
        pass_on(3)

        @pl.when(z % NY != 0)
        def _():
            shift_copy().wait_recv()

        @pl.when(z % NY == 0)
        def _():
            stay_copy().wait()

        for forward in (True, False):
            st_copy(1, forward, True).start()

    def event_2():
        q_copy(1).wait_recv()
        q_copy(4).wait_recv()
        pass_on(4)

    def event_3():
        q_copy(5).wait_recv()
        pass_on(5)

    def event_4():
        next_stretch(1)
        pass_on(6)

    def event_5():
        pass_on(7)

    def event_6():
        pass_on(8)

    def event_7():
        next_stretch(2)
        pass_on(9)

    def event_8():
        pass_on(10)

    def event_9():
        pass_on(11)

    def event_10():
        next_stretch(3)

    events = (
        event_0, event_1, event_2, event_3, event_4, event_5, event_6, event_7, event_8, event_9, event_10,
    )
    pass_on(0)
    pass_on(1)
    loads[OWN + 1].wait()
    score(0, 0, 0, 0)
    last = 11

    def one_turn(n, carry):
        for when, event in enumerate(events):
            pl.when(n == when)(event)
        a, step = turn(n)
        after, step_after = turn(n + 1)
        score(a, 1, step, 1)
        weigh(a, 0, step, 0)
        score(after, 0, step_after, 0)
        weigh(a, 1, step, 1)
        return carry

    lax.fori_loop(0, last, one_turn, 0)
    a, step = turn(last)
    score(a, 1, step, 1)
    weigh(a, 0, step, 0)
    weigh(a, 1, step, 1)

    def stretch(a, row):
        pairs = [(j - y + NY) % NY for j in range(row + 1)]
        keys = jnp.concatenate([st[pl.ds(2 * k, 2), pl.ds(0, TOK), :].reshape(2 * TOK, HD) for k in pairs], axis=0)
        vals = jnp.concatenate([st[2 * k + n, pl.ds(TOK, HD), :] for k in pairs for n in (0, 1)], axis=1)
        vals = jnp.concatenate([vals, jnp.ones((SUMS, 2 * TOK * (row + 1)), jnp.bfloat16)], axis=0)
        key = lax.broadcasted_iota(jnp.int32, (2 * TOK, TILE), 0)
        token = lax.broadcasted_iota(jnp.int32, (2 * TOK, TILE), 1) // GROUP
        key_pos = pairs[row] * TOK + key + jnp.where(key >= TOK, NY * TOK - TOK, 0)
        scored = []
        for half in (0, 1):
            s = lax.dot_general(keys, qs[columns(a, half), :], NT, preferred_element_type=jnp.float32)
            usable = key_pos <= z * TOK + half * (TILE // GROUP) + token
            own = jnp.where(usable, s[row * 2 * TOK:, :], LOWEST)
            scored.append(own if row == 0 else jnp.concatenate([s[:row * 2 * TOK, :], own], axis=0))
        for half in (0, 1):
            add(columns(a, half), scored[half], vals)

    def stretch_of(a):
        offset = jnp.where(a == 3, 2, jnp.where(a == 2, 3, a))
        mine_row = (y + offset) % NY
        for row in range(NY):
            pl.when(mine_row == row)(functools.partial(stretch, a, row))

    next_stretch(4)

    def stretch_turn(n, carry):
        stretch_of(jnp.where(n == 0, 3, n))
        return carry

    lax.fori_loop(0, 3, stretch_turn, 0)

    def finish(a, half):
        cols = columns(a, half)
        part = acc[:, cols]
        total = part[HD:HD + 1, :]
        return part[:HD, :] * (1.0 / total), top[:, cols] + jnp.log2(total)

    def join(parts):
        peak = functools.reduce(jnp.maximum, [level for _, level in parts])
        shares = [jnp.exp2(level - peak) for _, level in parts]
        total = functools.reduce(jnp.add, shares)
        result = functools.reduce(
            jnp.add, [part.astype(jnp.float32) * (share / total) for (part, _), share in zip(parts, shares)]
        )
        return result, peak + jnp.log2(total)

    def arrived(n):
        for copy in o_copies(n):
            copy.wait_recv()
        return oget[n], lget[n]

    def send(n, result, level):
        osend[n] = result.astype(jnp.bfloat16)
        lsend[n] = level
        for copy in o_copies(n):
            copy.start()

    pass_on(12)
    pass_on(13)
    order = (3, 1, 2, 0)
    score(order[0], 0, 3, 0)
    for n, a in enumerate(order):
        score(a, 1, 3, 1)
        weigh(a, 0, 3, 0)
        if n < 3:
            score(order[n + 1], 0, 3, 0)
        weigh(a, 1, 3, 1)
        if a == 3:
            send(0, *finish(3, 0))
            send(1, *finish(3, 1))
        if a == 1:
            send(3, *finish(1, 1))
        if a == 2:
            send(4, *finish(2, 0))
            send(2, *join([finish(1, 0), arrived(0)]))
            send(5, *join([finish(2, 1), arrived(1)]))
    stretch_of(0)

    for half in (0, 1):
        result, _ = join([finish(0, half), arrived(2 + half), arrived(4 + half)])
        out[pl.ds(half * TILE, TILE), :] = result.T.astype(jnp.bfloat16)

    for m in range(MSGS):
        for forward in (True, False):
            kv_copy(m, forward).wait_send()
    for n in range(6):
        q_copy(n).wait_send()
    for hop in (1, 2, 3, 4):
        for forward in (True, False):
            st_copy(hop, forward, True).wait_send()

    @pl.when(z % NY != 0)
    def _():
        shift_copy().wait_send()

    for n in range(6):
        for copy in o_copies(n):
            copy.wait_send()
    for d in range(1, HEADS):
        page_copy(d, me).wait_send()
        page_copy(d, (me - d + HEADS) % HEADS).wait_recv()
    own_pages().wait()


def body(queries, cache_kv, new_kv, cache_lengths, plan):
    smem = pl.BlockSpec(memory_space=pltpu.SMEM)
    hbm = pl.BlockSpec(memory_space=pltpu.HBM)
    out, moved = pl.pallas_call(
        kernel,
        out_shape=(
            jax.ShapeDtypeStruct((ROWS, HD), jnp.bfloat16),
            jax.ShapeDtypeStruct((HEADS, 4 * BLOCK, HD), jnp.bfloat16),
        ),
        in_specs=[smem, smem, hbm, hbm, hbm],
        out_specs=(pl.BlockSpec(memory_space=pltpu.VMEM), pl.BlockSpec(memory_space=pl.ANY)),
        scratch_shapes=[
            pltpu.VMEM((PIECES, PIECE + HD, HD), jnp.bfloat16),
            pltpu.VMEM((NZ + 1, TOK + HD, HD), jnp.bfloat16),
            pltpu.VMEM((SUMS, PIECES * PIECE), jnp.bfloat16),
            pltpu.VMEM((NY * ROWS, HD), jnp.bfloat16),
            pltpu.VMEM((HD + SUMS, NY * ROWS), jnp.float32),
            pltpu.VMEM((1, NY * ROWS), jnp.float32),
            pltpu.VMEM((2, STEP, TILE), jnp.float32),
            pltpu.VMEM((OWN, 2 * PIECE, HD), jnp.bfloat16),
            pltpu.VMEM((2 * TOK, HD), jnp.bfloat16),
            pltpu.VMEM((OWN + 1, 2 * PIECE, HD), jnp.float32),
            pltpu.VMEM((HEADS, 4 * BLOCK, HD), jnp.bfloat16),
            pltpu.VMEM((6, HD, TILE), jnp.bfloat16),
            pltpu.VMEM((6, 1, TILE), jnp.float32),
            pltpu.VMEM((6, HD, TILE), jnp.bfloat16),
            pltpu.VMEM((6, 1, TILE), jnp.float32),
            pltpu.SemaphoreType.DMA((OWN + 2,)),
            pltpu.SemaphoreType.DMA((PIECES,)),
            pltpu.SemaphoreType.DMA((PIECES,)),
            pltpu.SemaphoreType.DMA((4, 2)),
            pltpu.SemaphoreType.DMA((4, 2)),
            pltpu.SemaphoreType.DMA,
            pltpu.SemaphoreType.DMA,
            pltpu.SemaphoreType.DMA((6,)),
            pltpu.SemaphoreType.DMA((6,)),
            pltpu.SemaphoreType.DMA((6,)),
            pltpu.SemaphoreType.DMA((6,)),
            pltpu.SemaphoreType.DMA((6,)),
            pltpu.SemaphoreType.DMA((6,)),
            pltpu.SemaphoreType.DMA((HEADS,)),
            pltpu.SemaphoreType.DMA((HEADS,)),
            pltpu.SemaphoreType.DMA,
        ],
        compiler_params=pltpu.CompilerParams(
            collective_id=0, has_side_effects=True, vmem_limit_bytes=58 * 2 ** 20
        ),
        name="stretch_attention",
    )(
        cache_lengths,
        plan.reshape(PAGES),
        queries.reshape(ROWS, HD),
        cache_kv.reshape(2 * CACHE, HD),
        new_kv.reshape(2 * TOK, HD),
    )
    attended = out.reshape(TOK, 1, GROUP, HD)
    moved = moved.reshape(HEADS, 2, BLOCK, 2, HD)
    migrated = jnp.transpose(moved, (1, 2, 3, 0, 4)).reshape(1, 1, 2, BLOCK, 2, HEADS, HD)
    return attended, migrated


def solution(mesh):
    return jax.shard_map(
        body,
        mesh=mesh,
        in_specs=(
            P("ctx", ("head", "inst"), None, None),
            P("ctx", None, ("head", "inst"), None),
            P("ctx", None, ("head", "inst"), None),
            P(),
            P("ctx", None),
        ),
        out_specs=(
            P("ctx", ("head", "inst"), None, None),
            P("inst", "ctx", "head", None, None, None, None),
        ),
        check_vma=False,
    )
```

```python
import functools
import math

import jax
import jax.numpy as jnp
from jax import lax
from jax.experimental import pallas as pl
from jax.experimental.pallas import tpu as pltpu
from jax.sharding import PartitionSpec as P

MESH = pl.DeviceIdType.MESH
NY, NZ = 4, 8
NH, NI = 2, 4
HEADS = NH * NI
HD = 128
GROUP = 8
TOK = 128
ROWS = TOK * GROUP
CACHE = 512
PIECE = 128
OWN = CACHE // PIECE
MSGS = 14
PIECES = OWN + 2 * MSGS
MOST = 8
TILE = 512
BLOCK = 16
PAGES = TOK // BLOCK
CAP = PAGES // 2
SUMS = 16
SCALE = HD ** -0.5 * math.log2(math.e)
LOWEST = -1.0e30
NT = (((1,), (1,)), ((), ()))
OFFSETS = (0, 1, 3, 2)


def piece_of(m, forward):
    return OWN + 2 * m + (0 if forward else 1)


def quarter_of(m, forward):
    return (m + (0 if forward else 2)) % OWN


def shard_of(m, forward):
    hop = 1 + m // OWN
    return (-hop if forward else hop), quarter_of(m, forward)


def kernel(lens, plan, q_in, cache_in, fresh_in, out, moved,
           kv, st, live, qs, acc, top, sbuf, raw, fraw, wide, packed, landed, paged, osend, lsend, oget, lget,
           in_s, kv_s, kv_r, st_s, st_r, sh_s, sh_r, q_s, q_r, o_s, o_r, l_s, l_r, mg_s, mg_r, own_s):
    ctx = lax.axis_index("ctx")
    head = lax.axis_index("head")
    inst = lax.axis_index("inst")
    y, z = ctx // NZ, ctx % NZ
    me = head * NI + inst

    def at_z(d):
        return (y * NZ + (z + d + NZ) % NZ, head, inst)

    def at_y(d):
        return (((y + d + NY) % NY) * NZ + z, head, inst)

    def at_head(h):
        return (ctx, h // NI, h % NI)

    loads = [
        pltpu.make_async_copy(cache_in.at[pl.ds(n * 2 * PIECE, 2 * PIECE)], raw.at[n], in_s.at[n])
        for n in range(OWN)
    ]
    loads.append(pltpu.make_async_copy(fresh_in, fraw, in_s.at[OWN]))
    loads.append(pltpu.make_async_copy(q_in, qs.at[pl.ds(0, ROWS)], in_s.at[OWN + 1]))
    for load in loads:
        load.start()

    barrier = pltpu.get_barrier_semaphore()
    peers = [at_z(1), at_z(-1), at_y(1), at_y(2), at_y(3)]
    peers += [at_head((me + d) % HEADS) for d in range(1, HEADS)]
    for peer in peers:
        pl.semaphore_signal(barrier, inc=1, device_id=peer, device_id_type=MESH)

    def kv_copy(m, forward):
        src = quarter_of(m, forward) if m < OWN else piece_of(m - OWN, forward)
        dst = piece_of(m, forward)
        return pltpu.make_async_remote_copy(
            src_ref=kv.at[src],
            dst_ref=kv.at[dst],
            send_sem=kv_s.at[dst],
            recv_sem=kv_r.at[dst],
            device_id=at_z(1 if forward else -1),
            device_id_type=MESH,
        )

    def arrive(*messages):
        for m in messages:
            for forward in (True, False):
                kv_copy(m, forward).wait_recv()

    def pass_on(*messages):
        for m in messages:
            for forward in (True, False):
                kv_copy(m + OWN, forward).start()

    def q_copy(n):
        half = (0, 1, 0, 1, 0, 1)[n]
        src = (0, 0, 0, 0, 2, 1)[n]
        dst = (2, 2, 1, 1, 3, 3)[n]
        to = (1, 1, -1, -1, 1, -1)[n]
        if n < 4:
            src_ref = q_in.at[pl.ds(half * TILE, TILE)]
        else:
            src_ref = qs.at[pl.ds(src * ROWS + half * TILE, TILE)]
        return pltpu.make_async_remote_copy(
            src_ref=src_ref,
            dst_ref=qs.at[pl.ds(dst * ROWS + half * TILE, TILE)],
            send_sem=q_s.at[n],
            recv_sem=q_r.at[n],
            device_id=at_y(to),
            device_id_type=MESH,
        )

    def place(zz):
        zz = (zz + NZ) % NZ
        return (zz % NY) * 2 + zz // NY

    def shift_copy():
        return pltpu.make_async_remote_copy(
            src_ref=st.at[NZ],
            dst_ref=st.at[place(z)],
            send_sem=sh_s,
            recv_sem=sh_r,
            device_id=(((y - z + NZ) % NY) * NZ + z, head, inst),
            device_id_type=MESH,
        )

    def stay_copy():
        return pltpu.make_async_copy(st.at[NZ], st.at[place(z)], sh_r)

    def st_ref(zz, hop, forward):
        if hop < 4:
            return st.at[place(zz)]
        return st.at[place(zz), pl.ds(0 if forward else TOK, TOK)]

    def st_copy(hop, forward, sending):
        sign = 1 if forward else -1
        ref = st_ref(z - sign * (hop - 1 if sending else hop), hop, forward)
        return pltpu.make_async_remote_copy(
            src_ref=ref,
            dst_ref=ref,
            send_sem=st_s.at[hop - 1, int(forward)],
            recv_sem=st_r.at[hop - 1, int(forward)],
            device_id=at_z(sign),
            device_id_type=MESH,
        )

    def next_stretch(hop):
        for forward in (True, False):
            st_copy(hop, forward, False).wait_recv()
            if hop < 4:
                st_copy(hop + 1, forward, True).start()

    def page_copy(d, dst):
        to = (me + d) % HEADS
        return pltpu.make_async_remote_copy(
            src_ref=packed.at[(to % NI) * NH + to // NI],
            dst_ref=landed.at[dst],
            send_sem=mg_s.at[d],
            recv_sem=mg_r.at[d],
            device_id=at_head(to),
            device_id_type=MESH,
        )

    def own_pages():
        return pltpu.make_async_copy(packed.at[inst * NH + head], landed.at[me], own_s)

    def o_copies(n):
        to = at_y((1, -1, 1, 1, -1, -1)[n])
        return (
            pltpu.make_async_remote_copy(
                src_ref=osend.at[n], dst_ref=oget.at[n], send_sem=o_s.at[n], recv_sem=o_r.at[n],
                device_id=to, device_id_type=MESH,
            ),
            pltpu.make_async_remote_copy(
                src_ref=lsend.at[n], dst_ref=lget.at[n], send_sem=l_s.at[n], recv_sem=l_r.at[n],
                device_id=to, device_id_type=MESH,
            ),
        )

    length = lens[ctx]

    def split(n):
        return wide[n, pl.ds(0, PIECE, stride=2), :], wide[n, pl.ds(1, PIECE, stride=2), :]

    def own_piece(n, first):
        loads[n].wait()
        wide[n] = raw[n].astype(jnp.float32)
        keys, values = split(n)
        first = keys[0:1, :] if n == 0 else first
        usable = lax.broadcasted_iota(jnp.int32, (PIECE, HD), 0) + n * PIECE < length
        kv[n, pl.ds(0, PIECE), :] = jnp.where(usable, keys, jnp.broadcast_to(first, (PIECE, HD))).astype(jnp.bfloat16)
        kv[n, pl.ds(PIECE, HD), :] = jnp.where(usable, values, 0.0).T.astype(jnp.bfloat16)
        return first

    first = own_piece(0, None)
    pl.semaphore_wait(barrier, len(peers))
    kv_copy(0, True).start()
    loads[OWN].wait()
    fresh = fraw[...].astype(jnp.float32)
    wide[OWN] = fresh
    keys, values = split(OWN)
    st[NZ, pl.ds(0, TOK), :] = keys.astype(jnp.bfloat16)
    st[NZ, pl.ds(TOK, HD), :] = values.T.astype(jnp.bfloat16)

    @pl.when(z % NY != 0)
    def _():
        shift_copy().start()

    @pl.when(z % NY == 0)
    def _():
        stay_copy().start()

    for n in (0, 2, 1, 3):
        q_copy(n).start()
    own_piece(2, first)
    kv_copy(0, False).start()
    own_piece(1, first)
    kv_copy(1, True).start()
    own_piece(3, first)
    kv_copy(1, False).start()
    for forward in (True, False):
        kv_copy(2, forward).start()

    def empty(n, carry):
        acc[:, pl.ds(pl.multiple_of(n * TILE, TILE), TILE)] = jnp.zeros((HD + SUMS, TILE), jnp.float32)
        return carry

    lax.fori_loop(0, NY * ROWS // TILE, empty, 0)
    top[...] = jnp.full((1, NY * ROWS), LOWEST, jnp.float32)
    origin = {n: (0, n) for n in range(OWN)}
    for m in range(MSGS):
        for forward in (True, False):
            origin[piece_of(m, forward)] = shard_of(m, forward)
    lane = lax.broadcasted_iota(jnp.int32, (SUMS, PIECE), 1)
    for n in range(PIECES):
        d, quarter = origin[n]
        filled = lens[y * NZ + (z + d + NZ) % NZ]
        live[:, pl.ds(n * PIECE, PIECE)] = jnp.where(lane + quarter * PIECE < filled, 1.0, 0.0).astype(jnp.bfloat16)

    targets = []
    for b in range(PAGES):
        earlier = jnp.int32(0)
        for a in range(b):
            earlier = earlier + (plan[a] == plan[b]).astype(jnp.int32)
        targets.append(plan[b] * CAP + earlier)
    for t in range(NI * CAP):
        page = jnp.zeros((2 * BLOCK, HD), jnp.float32)
        for b in range(PAGES):
            page = page + fresh[2 * BLOCK * b:2 * BLOCK * (b + 1), :] * (targets[b] == t).astype(jnp.float32)
        packed[t // 2, pl.ds((t % 2) * 2 * BLOCK, 2 * BLOCK), :] = page.astype(jnp.bfloat16)
    for d in range(1, HEADS):
        page_copy(d, me).start()
    own_pages().start()

    @pl.when(z % NY != 0)
    def _():
        shift_copy().wait_recv()

    @pl.when(z % NY == 0)
    def _():
        stay_copy().wait()

    for forward in (True, False):
        st_copy(1, forward, True).start()
    for forward in (True, False):
        kv_copy(3, forward).start()

    def columns(a, half):
        return pl.ds(pl.multiple_of(a * ROWS + half * TILE, TILE), TILE)

    def add(cols, scores, vals):
        before = top[:, cols]
        peak = jnp.maximum(before, jnp.max(scores, axis=0, keepdims=True) * SCALE)
        weights = jnp.exp2(scores * SCALE - peak).astype(jnp.bfloat16)
        part = jnp.dot(vals, weights, preferred_element_type=jnp.float32)
        acc[:, cols] = acc[:, cols] * jnp.exp2(before - peak) + part
        top[:, cols] = peak

    def score(a, half, start, count, slot):
        keys = kv[pl.ds(start, count), pl.ds(0, PIECE), :].reshape(count * PIECE, HD)
        sbuf[slot, pl.ds(0, count * PIECE), :] = lax.dot_general(
            keys, qs[columns(a, half), :], NT, preferred_element_type=jnp.float32
        )

    def weigh(a, half, start, count, slot):
        vals = jnp.concatenate([kv[start + n, pl.ds(PIECE, HD), :] for n in range(count)], axis=1)
        sums = live[:, pl.ds(pl.multiple_of(start * PIECE, PIECE), count * PIECE)]
        scores = sbuf[slot, pl.ds(0, count * PIECE), :]
        add(columns(a, half), scores, jnp.concatenate([vals, sums], axis=0))

    first_turns = (
        ((0, 0, 0), (0, 1, 0)),
        ((1, 0, 0), (2, 0, 0)),
        ((1, 1, 0), (2, 1, 0)),
        ((1, 0, 8), (1, 1, 8)),
        ((2, 0, 8), (2, 1, 8)),
        ((3, 0, 0), (3, 1, 0)),
        ((3, 0, 8), (3, 1, 8)),
    )
    second_turns = tuple(((a, 0, start), (a, 1, start)) for start in (16, 20) for a in (3, 1, 2))
    own_turns = tuple(((0, 0, start), (0, 1, start)) for start in (8, 16, 24))

    def event_0():
        q_copy(2).wait_recv()

    def event_1():
        q_copy(0).wait_recv()
        q_copy(4).start()
        next_stretch(1)
        arrive(2)
        pass_on(2)
        q_copy(3).wait_recv()
        q_copy(5).start()
        arrive(3)
        pass_on(3)

    def event_2():
        q_copy(1).wait_recv()
        arrive(4, 5)

    def event_4():
        next_stretch(2)
        pass_on(4, 5)
        q_copy(4).wait_recv()
        q_copy(5).wait_recv()

    def turns(table, count, events):
        def tile(n, u):
            found = [jnp.int32(value) for value in table[0][u]]
            for when in range(1, len(table)):
                found = [jnp.where(n == when, value, old) for value, old in zip(table[when][u], found)]
            return found

        def one_turn(n, carry):
            for when, event in events.items():
                pl.when(n == when)(event)
            one, two, after = tile(n, 0), tile(n, 1), tile(n + 1, 0)
            score(*two, count, 1)
            weigh(*one, count, 0)
            score(*after, count, 0)
            weigh(*two, count, 1)
            return carry

        score(*table[0][0], count, 0)
        lax.fori_loop(0, len(table) - 1, one_turn, 0)
        one, two = table[-1]
        score(*two, count, 1)
        weigh(*one, count, 0)
        weigh(*two, count, 1)

    arrive(0, 1)
    pass_on(0, 1)
    loads[OWN + 1].wait()
    turns(first_turns, 8, {0: event_0, 1: event_1, 2: event_2, 4: event_4})
    arrive(6, 7)

    def event_second_0():
        next_stretch(3)
        pass_on(6, 7)

    def event_second_2():
        arrive(8, 9)
        pass_on(8, 9)

    turns(second_turns, 4, {0: event_second_0, 2: event_second_2})

    for d in range(1, HEADS):
        page_copy(d, (me - d + HEADS) % HEADS).wait_recv()
    own_pages().wait()
    for h in range(HEADS):
        paged[pl.ds(h, 4 * BLOCK, stride=HEADS), :] = landed[h].astype(jnp.float32)
    moved[...] = paged[...].astype(jnp.bfloat16)

    def stretch(a, row):
        pairs = [(j - y + NY) % NY for j in range(row + 1)]
        keys = jnp.concatenate([st[pl.ds(2 * k, 2), pl.ds(0, TOK), :].reshape(2 * TOK, HD) for k in pairs], axis=0)
        vals = jnp.concatenate([st[2 * k + n, pl.ds(TOK, HD), :] for k in pairs for n in (0, 1)], axis=1)
        vals = jnp.concatenate([vals, jnp.ones((SUMS, 2 * TOK * (row + 1)), jnp.bfloat16)], axis=0)
        key = lax.broadcasted_iota(jnp.int32, (2 * TOK, TILE), 0)
        token = lax.broadcasted_iota(jnp.int32, (2 * TOK, TILE), 1) // GROUP
        key_pos = pairs[row] * TOK + key + jnp.where(key >= TOK, NY * TOK - TOK, 0)
        scored = []
        for half in (0, 1):
            s = lax.dot_general(keys, qs[columns(a, half), :], NT, preferred_element_type=jnp.float32)
            usable = key_pos <= z * TOK + half * (TILE // GROUP) + token
            own = jnp.where(usable, s[row * 2 * TOK:, :], LOWEST)
            scored.append(own if row == 0 else jnp.concatenate([s[:row * 2 * TOK, :], own], axis=0))
        for half in (0, 1):
            add(columns(a, half), scored[half], vals)

    def stretch_of(a):
        offset = jnp.where(a == 3, 2, jnp.where(a == 2, 3, a))
        mine_row = (y + offset) % NY
        for row in range(NY):
            pl.when(mine_row == row)(functools.partial(stretch, a, row))

    next_stretch(4)

    def stretch_turn(n, carry):
        stretch_of(jnp.where(n == 0, 3, n))
        return carry

    lax.fori_loop(0, 3, stretch_turn, 0)

    def finish(a, half):
        cols = columns(a, half)
        part = acc[:, cols]
        total = part[HD:HD + 1, :]
        return part[:HD, :] * (1.0 / total), top[:, cols] + jnp.log2(total)

    def join(parts):
        peak = functools.reduce(jnp.maximum, [level for _, level in parts])
        shares = [jnp.exp2(level - peak) for _, level in parts]
        total = functools.reduce(jnp.add, shares)
        result = functools.reduce(
            jnp.add, [part.astype(jnp.float32) * (share / total) for (part, _), share in zip(parts, shares)]
        )
        return result, peak + jnp.log2(total)

    def arrived(n):
        for copy in o_copies(n):
            copy.wait_recv()
        return oget[n], lget[n]

    def send(n, result, level):
        osend[n] = result.astype(jnp.bfloat16)
        lsend[n] = level
        for copy in o_copies(n):
            copy.start()

    arrive(10, 11, 12, 13)
    order = ((3, 0), (3, 1), (1, 1), (2, 0), (1, 0), (2, 1))
    score(*order[0], 24, 8, 0)
    for n, (a, half) in enumerate(order):
        if n + 1 < len(order):
            score(*order[n + 1], 24, 8, (n + 1) % 2)
        weigh(a, half, 24, 8, n % 2)
        if n == 1:
            send(0, *finish(3, 0))
            send(1, *finish(3, 1))
        if n == 3:
            send(3, *finish(1, 1))
            send(4, *finish(2, 0))
        if n == 5:
            send(2, *join([finish(1, 0), arrived(0)]))
            send(5, *join([finish(2, 1), arrived(1)]))
    turns(own_turns, 8, {})
    stretch_of(0)

    for half in (0, 1):
        result, _ = join([finish(0, half), arrived(2 + half), arrived(4 + half)])
        out[pl.ds(half * TILE, TILE), :] = result.T.astype(jnp.bfloat16)

    for m in range(MSGS):
        for forward in (True, False):
            kv_copy(m, forward).wait_send()
    for n in range(6):
        q_copy(n).wait_send()
    for hop in (1, 2, 3, 4):
        for forward in (True, False):
            st_copy(hop, forward, True).wait_send()

    @pl.when(z % NY != 0)
    def _():
        shift_copy().wait_send()

    for n in range(6):
        for copy in o_copies(n):
            copy.wait_send()
    for d in range(1, HEADS):
        page_copy(d, me).wait_send()


def body(queries, cache_kv, new_kv, cache_lengths, plan):
    smem = pl.BlockSpec(memory_space=pltpu.SMEM)
    hbm = pl.BlockSpec(memory_space=pltpu.HBM)
    out, moved = pl.pallas_call(
        kernel,
        out_shape=(
            jax.ShapeDtypeStruct((ROWS, HD), jnp.bfloat16),
            jax.ShapeDtypeStruct((4 * BLOCK * HEADS, HD), jnp.bfloat16),
        ),
        in_specs=[smem, smem, hbm, hbm, hbm],
        out_specs=(pl.BlockSpec(memory_space=pltpu.VMEM),) * 2,
        scratch_shapes=[
            pltpu.VMEM((PIECES, PIECE + HD, HD), jnp.bfloat16),
            pltpu.VMEM((NZ + 1, TOK + HD, HD), jnp.bfloat16),
            pltpu.VMEM((SUMS, PIECES * PIECE), jnp.bfloat16),
            pltpu.VMEM((NY * ROWS, HD), jnp.bfloat16),
            pltpu.VMEM((HD + SUMS, NY * ROWS), jnp.float32),
            pltpu.VMEM((1, NY * ROWS), jnp.float32),
            pltpu.VMEM((2, MOST * PIECE, TILE), jnp.float32),
            pltpu.VMEM((OWN, 2 * PIECE, HD), jnp.bfloat16),
            pltpu.VMEM((2 * TOK, HD), jnp.bfloat16),
            pltpu.VMEM((OWN + 1, 2 * PIECE, HD), jnp.float32),
            pltpu.VMEM((HEADS, 4 * BLOCK, HD), jnp.bfloat16),
            pltpu.VMEM((HEADS, 4 * BLOCK, HD), jnp.bfloat16),
            pltpu.VMEM((4 * BLOCK * HEADS, HD), jnp.float32),
            pltpu.VMEM((6, HD, TILE), jnp.bfloat16),
            pltpu.VMEM((6, 1, TILE), jnp.float32),
            pltpu.VMEM((6, HD, TILE), jnp.bfloat16),
            pltpu.VMEM((6, 1, TILE), jnp.float32),
            pltpu.SemaphoreType.DMA((OWN + 2,)),
            pltpu.SemaphoreType.DMA((PIECES,)),
            pltpu.SemaphoreType.DMA((PIECES,)),
            pltpu.SemaphoreType.DMA((4, 2)),
            pltpu.SemaphoreType.DMA((4, 2)),
            pltpu.SemaphoreType.DMA,
            pltpu.SemaphoreType.DMA,
            pltpu.SemaphoreType.DMA((6,)),
            pltpu.SemaphoreType.DMA((6,)),
            pltpu.SemaphoreType.DMA((6,)),
            pltpu.SemaphoreType.DMA((6,)),
            pltpu.SemaphoreType.DMA((6,)),
            pltpu.SemaphoreType.DMA((6,)),
            pltpu.SemaphoreType.DMA((HEADS,)),
            pltpu.SemaphoreType.DMA((HEADS,)),
            pltpu.SemaphoreType.DMA,
        ],
        compiler_params=pltpu.CompilerParams(
            collective_id=0, has_side_effects=True, vmem_limit_bytes=32 * 2 ** 20
        ),
        name="stretch_attention",
    )(
        cache_lengths,
        plan.reshape(PAGES),
        *(pltpu.with_memory_space_constraint(x, pltpu.HBM) for x in (
            queries.reshape(ROWS, HD),
            cache_kv.reshape(2 * CACHE, HD),
            new_kv.reshape(2 * TOK, HD),
        )),
    )
    attended = out.reshape(TOK, 1, GROUP, HD)
    migrated = moved.reshape(1, 1, 2, BLOCK, 2, HEADS, HD)
    return attended, migrated


def solution(mesh):
    return jax.shard_map(
        body,
        mesh=mesh,
        in_specs=(
            P("ctx", ("head", "inst"), None, None),
            P("ctx", None, ("head", "inst"), None),
            P("ctx", None, ("head", "inst"), None),
            P(),
            P("ctx", None),
        ),
        out_specs=(
            P("ctx", ("head", "inst"), None, None),
            P("inst", "ctx", "head", None, None, None, None),
        ),
        check_vma=False,
    )
```

```python
import functools
import math

import jax
import jax.numpy as jnp
from jax import lax
from jax.experimental import pallas as pl
from jax.experimental.pallas import tpu as pltpu
from jax.sharding import PartitionSpec as P

MESH = pl.DeviceIdType.MESH
NY, NZ = 4, 8
NH, NI = 2, 4
HEADS = NH * NI
HD = 128
GROUP = 8
TOK = 128
ROWS = TOK * GROUP
CACHE = 512
PIECE = 128
OWN = CACHE // PIECE
MSGS = 14
PIECES = OWN + 2 * MSGS
MOST = 8
TILE = 512
BLOCK = 16
PAGES = TOK // BLOCK
CAP = PAGES // 2
SUMS = 16
SCALE = HD ** -0.5 * math.log2(math.e)
LOWEST = -1.0e30
NT = (((1,), (1,)), ((), ()))
OFFSETS = (0, 1, 3, 2)


def piece_of(m, forward):
    return OWN + 2 * m + (0 if forward else 1)


def quarter_of(m, forward):
    return (m + (0 if forward else 2)) % OWN


def shard_of(m, forward):
    hop = 1 + m // OWN
    return (-hop if forward else hop), quarter_of(m, forward)


def kernel(lens, plan, q_in, cache_in, fresh_in, out, moved,
           kv, st, live, qs, acc, top, sbuf, raw, fraw, wide, packed, landed, paged, osend, lsend, oget, lget,
           in_s, kv_s, kv_r, st_s, st_r, sh_s, sh_r, q_s, q_r, o_s, o_r, l_s, l_r, mg_s, mg_r, own_s):
    ctx = lax.axis_index("ctx")
    head = lax.axis_index("head")
    inst = lax.axis_index("inst")
    y, z = ctx // NZ, ctx % NZ
    me = head * NI + inst

    def at_z(d):
        return (y * NZ + (z + d + NZ) % NZ, head, inst)

    def at_y(d):
        return (((y + d + NY) % NY) * NZ + z, head, inst)

    def at_head(h):
        return (ctx, h // NI, h % NI)

    loads = [
        pltpu.make_async_copy(cache_in.at[pl.ds(n * 2 * PIECE, 2 * PIECE)], raw.at[n], in_s.at[n])
        for n in range(OWN)
    ]
    loads.append(pltpu.make_async_copy(fresh_in, fraw, in_s.at[OWN]))
    loads.append(pltpu.make_async_copy(q_in, qs.at[pl.ds(0, ROWS)], in_s.at[OWN + 1]))
    loads[0].start()

    barrier = pltpu.get_barrier_semaphore()
    peers = [at_z(1), at_z(-1), at_y(1), at_y(2), at_y(3)]
    peers += [at_head((me + d) % HEADS) for d in range(1, HEADS)]
    for peer in peers:
        pl.semaphore_signal(barrier, inc=1, device_id=peer, device_id_type=MESH)
    for n in (OWN, 2, 1, 3, OWN + 1):
        loads[n].start()

    def kv_copy(m, forward):
        src = quarter_of(m, forward) if m < OWN else piece_of(m - OWN, forward)
        dst = piece_of(m, forward)
        return pltpu.make_async_remote_copy(
            src_ref=kv.at[src],
            dst_ref=kv.at[dst],
            send_sem=kv_s.at[dst],
            recv_sem=kv_r.at[dst],
            device_id=at_z(1 if forward else -1),
            device_id_type=MESH,
        )

    def arrive(*messages):
        for m in messages:
            for forward in (True, False):
                kv_copy(m, forward).wait_recv()

    def pass_on(*messages):
        for m in messages:
            for forward in (True, False):
                kv_copy(m + OWN, forward).start()

    def q_copy(n):
        half = (0, 1, 0, 1, 0, 1)[n]
        src = (0, 0, 0, 0, 2, 1)[n]
        dst = (2, 2, 1, 1, 3, 3)[n]
        to = (1, 1, -1, -1, 1, -1)[n]
        if n < 4:
            src_ref = q_in.at[pl.ds(half * TILE, TILE)]
        else:
            src_ref = qs.at[pl.ds(src * ROWS + half * TILE, TILE)]
        return pltpu.make_async_remote_copy(
            src_ref=src_ref,
            dst_ref=qs.at[pl.ds(dst * ROWS + half * TILE, TILE)],
            send_sem=q_s.at[n],
            recv_sem=q_r.at[n],
            device_id=at_y(to),
            device_id_type=MESH,
        )

    def place(zz):
        zz = (zz + NZ) % NZ
        return (zz % NY) * 2 + zz // NY

    def shift_copy():
        return pltpu.make_async_remote_copy(
            src_ref=st.at[NZ],
            dst_ref=st.at[place(z)],
            send_sem=sh_s,
            recv_sem=sh_r,
            device_id=(((y - z + NZ) % NY) * NZ + z, head, inst),
            device_id_type=MESH,
        )

    def stay_copy():
        return pltpu.make_async_copy(st.at[NZ], st.at[place(z)], sh_r)

    def st_ref(zz, hop, forward):
        if hop < 4:
            return st.at[place(zz)]
        return st.at[place(zz), pl.ds(0 if forward else TOK, TOK)]

    def st_copy(hop, forward, sending):
        sign = 1 if forward else -1
        ref = st_ref(z - sign * (hop - 1 if sending else hop), hop, forward)
        return pltpu.make_async_remote_copy(
            src_ref=ref,
            dst_ref=ref,
            send_sem=st_s.at[hop - 1, int(forward)],
            recv_sem=st_r.at[hop - 1, int(forward)],
            device_id=at_z(sign),
            device_id_type=MESH,
        )

    def next_stretch(hop):
        for forward in (True, False):
            st_copy(hop, forward, False).wait_recv()
            if hop < 4:
                st_copy(hop + 1, forward, True).start()

    def page_copy(d, dst):
        to = (me + d) % HEADS
        return pltpu.make_async_remote_copy(
            src_ref=packed.at[(to % NI) * NH + to // NI],
            dst_ref=landed.at[dst],
            send_sem=mg_s.at[d],
            recv_sem=mg_r.at[d],
            device_id=at_head(to),
            device_id_type=MESH,
        )

    def own_pages():
        return pltpu.make_async_copy(packed.at[inst * NH + head], landed.at[me], own_s)

    def o_copies(n):
        to = at_y((1, -1, 1, 1, -1, -1)[n])
        return (
            pltpu.make_async_remote_copy(
                src_ref=osend.at[n], dst_ref=oget.at[n], send_sem=o_s.at[n], recv_sem=o_r.at[n],
                device_id=to, device_id_type=MESH,
            ),
            pltpu.make_async_remote_copy(
                src_ref=lsend.at[n], dst_ref=lget.at[n], send_sem=l_s.at[n], recv_sem=l_r.at[n],
                device_id=to, device_id_type=MESH,
            ),
        )

    length = lens[ctx]

    def split(n):
        return wide[n, pl.ds(0, PIECE, stride=2), :], wide[n, pl.ds(1, PIECE, stride=2), :]

    def own_piece(n, first):
        loads[n].wait()
        wide[n] = raw[n].astype(jnp.float32)
        keys, values = split(n)
        first = keys[0:1, :] if n == 0 else first
        usable = lax.broadcasted_iota(jnp.int32, (PIECE, HD), 0) + n * PIECE < length
        kv[n, pl.ds(0, PIECE), :] = jnp.where(usable, keys, jnp.broadcast_to(first, (PIECE, HD))).astype(jnp.bfloat16)
        kv[n, pl.ds(PIECE, HD), :] = jnp.where(usable, values, 0.0).T.astype(jnp.bfloat16)
        return first

    first = own_piece(0, None)
    pl.semaphore_wait(barrier, len(peers))
    kv_copy(0, True).start()
    loads[OWN].wait()
    fresh = fraw[...].astype(jnp.float32)
    wide[OWN] = fresh
    keys, values = split(OWN)
    st[NZ, pl.ds(0, TOK), :] = keys.astype(jnp.bfloat16)
    st[NZ, pl.ds(TOK, HD), :] = values.T.astype(jnp.bfloat16)

    @pl.when(z % NY != 0)
    def _():
        shift_copy().start()

    @pl.when(z % NY == 0)
    def _():
        stay_copy().start()

    for n in (0, 2, 1, 3):
        q_copy(n).start()
    own_piece(2, first)
    kv_copy(0, False).start()
    own_piece(1, first)
    kv_copy(1, True).start()
    own_piece(3, first)
    kv_copy(1, False).start()
    for forward in (True, False):
        kv_copy(2, forward).start()

    def empty(n, carry):
        acc[:, pl.ds(pl.multiple_of(n * TILE, TILE), TILE)] = jnp.zeros((HD + SUMS, TILE), jnp.float32)
        return carry

    lax.fori_loop(0, NY * ROWS // TILE, empty, 0)
    top[...] = jnp.full((1, NY * ROWS), LOWEST, jnp.float32)
    origin = {n: (0, n) for n in range(OWN)}
    for m in range(MSGS):
        for forward in (True, False):
            origin[piece_of(m, forward)] = shard_of(m, forward)
    lane = lax.broadcasted_iota(jnp.int32, (SUMS, PIECE), 1)
    for n in range(PIECES):
        d, quarter = origin[n]
        filled = lens[y * NZ + (z + d + NZ) % NZ]
        live[:, pl.ds(n * PIECE, PIECE)] = jnp.where(lane + quarter * PIECE < filled, 1.0, 0.0).astype(jnp.bfloat16)

    targets = []
    for b in range(PAGES):
        earlier = jnp.int32(0)
        for a in range(b):
            earlier = earlier + (plan[a] == plan[b]).astype(jnp.int32)
        targets.append(plan[b] * CAP + earlier)
    for t in range(NI * CAP):
        page = jnp.zeros((2 * BLOCK, HD), jnp.float32)
        for b in range(PAGES):
            page = page + fresh[2 * BLOCK * b:2 * BLOCK * (b + 1), :] * (targets[b] == t).astype(jnp.float32)
        packed[t // 2, pl.ds((t % 2) * 2 * BLOCK, 2 * BLOCK), :] = page.astype(jnp.bfloat16)
    for d in range(1, HEADS):
        page_copy(d, me).start()
    own_pages().start()

    @pl.when(z % NY != 0)
    def _():
        shift_copy().wait_recv()

    @pl.when(z % NY == 0)
    def _():
        stay_copy().wait()

    for forward in (True, False):
        st_copy(1, forward, True).start()
    for forward in (True, False):
        kv_copy(3, forward).start()

    def columns(a, half):
        return pl.ds(pl.multiple_of(a * ROWS + half * TILE, TILE), TILE)

    def add(cols, scores, vals):
        before = top[:, cols]
        peak = jnp.maximum(before, jnp.max(scores, axis=0, keepdims=True) * SCALE)
        weights = jnp.exp2(scores * SCALE - peak).astype(jnp.bfloat16)
        part = jnp.dot(vals, weights, preferred_element_type=jnp.float32)
        acc[:, cols] = acc[:, cols] * jnp.exp2(before - peak) + part
        top[:, cols] = peak

    def score(a, half, start, count, slot):
        keys = kv[pl.ds(start, count), pl.ds(0, PIECE), :].reshape(count * PIECE, HD)
        sbuf[slot, pl.ds(0, count * PIECE), :] = lax.dot_general(
            keys, qs[columns(a, half), :], NT, preferred_element_type=jnp.float32
        )

    def weigh(a, half, start, count, slot):
        vals = jnp.concatenate([kv[start + n, pl.ds(PIECE, HD), :] for n in range(count)], axis=1)
        sums = live[:, pl.ds(pl.multiple_of(start * PIECE, PIECE), count * PIECE)]
        scores = sbuf[slot, pl.ds(0, count * PIECE), :]
        add(columns(a, half), scores, jnp.concatenate([vals, sums], axis=0))

    first_turns = (
        ((0, 0, 0), (0, 1, 0)),
        ((1, 0, 0), (2, 0, 0)),
        ((1, 1, 0), (2, 1, 0)),
    )
    more_turns = (
        ((1, 0, 8), (1, 1, 8)),
        ((2, 0, 8), (2, 1, 8)),
        ((3, 0, 0), (3, 1, 0)),
        ((3, 0, 8), (3, 1, 8)),
    )
    def whole(start, *shards):
        return tuple(((a, 0, start), (a, 1, start)) for a in shards)

    def event_0():
        q_copy(2).wait_recv()

    def event_1():
        q_copy(0).wait_recv()
        q_copy(4).start()
        next_stretch(1)
        arrive(2)
        pass_on(2)
        q_copy(3).wait_recv()
        q_copy(5).start()
        q_copy(1).wait_recv()
        arrive(3)
        pass_on(3)

    def event_4():
        next_stretch(2)
        pass_on(4, 5)
        q_copy(4).wait_recv()
        q_copy(5).wait_recv()

    def turns(table, count, events):
        def tile(n, u):
            found = [jnp.int32(value) for value in table[0][u]]
            for when in range(1, len(table)):
                found = [jnp.where(n == when, value, old) for value, old in zip(table[when][u], found)]
            return found

        def one_turn(n, carry):
            for when, event in events.items():
                pl.when(n == when)(event)
            one, two, after = tile(n, 0), tile(n, 1), tile(n + 1, 0)
            score(*two, count, 1)
            weigh(*one, count, 0)
            score(*after, count, 0)
            weigh(*two, count, 1)
            return carry

        score(*table[0][0], count, 0)
        lax.fori_loop(0, len(table) - 1, one_turn, 0)
        one, two = table[-1]
        score(*two, count, 1)
        weigh(*one, count, 0)
        weigh(*two, count, 1)

    arrive(0, 1)
    pass_on(0, 1)
    loads[OWN + 1].wait()
    turns(first_turns, 8, {0: event_0, 1: event_1})
    turns(whole(8, 0), 4, {})
    arrive(4, 5)
    turns(more_turns, 8, {1: event_4})
    arrive(6, 7)

    def event_third():
        next_stretch(3)
        pass_on(6, 7)

    turns(whole(16, 3, 1, 2), 4, {1: event_third})
    arrive(8, 9)
    pass_on(8, 9)
    turns(whole(20, 3, 1, 2), 4, {})

    def stretch(a, row):
        pairs = [(j - y + NY) % NY for j in range(row + 1)]
        keys = jnp.concatenate([st[pl.ds(2 * k, 2), pl.ds(0, TOK), :].reshape(2 * TOK, HD) for k in pairs], axis=0)
        vals = jnp.concatenate([st[2 * k + n, pl.ds(TOK, HD), :] for k in pairs for n in (0, 1)], axis=1)
        vals = jnp.concatenate([vals, jnp.ones((SUMS, 2 * TOK * (row + 1)), jnp.bfloat16)], axis=0)
        key = lax.broadcasted_iota(jnp.int32, (2 * TOK, TILE), 0)
        token = lax.broadcasted_iota(jnp.int32, (2 * TOK, TILE), 1) // GROUP
        key_pos = pairs[row] * TOK + key + jnp.where(key >= TOK, NY * TOK - TOK, 0)
        scored = []
        for half in (0, 1):
            s = lax.dot_general(keys, qs[columns(a, half), :], NT, preferred_element_type=jnp.float32)
            usable = key_pos <= z * TOK + half * (TILE // GROUP) + token
            own = jnp.where(usable, s[row * 2 * TOK:, :], LOWEST)
            scored.append(own if row == 0 else jnp.concatenate([s[:row * 2 * TOK, :], own], axis=0))
        for half in (0, 1):
            add(columns(a, half), scored[half], vals)

    def stretch_of(a):
        offset = jnp.where(a == 3, 2, jnp.where(a == 2, 3, a))
        mine_row = (y + offset) % NY
        for row in range(NY):
            pl.when(mine_row == row)(functools.partial(stretch, a, row))

    next_stretch(4)

    def third_step():
        arrive(10, 11)
        turns(whole(24, 3), 4, {})

    def stretch_turn(n, carry):
        pl.when(n == 1)(third_step)
        stretch_of(jnp.where(n == 0, 3, 1))
        return carry

    lax.fori_loop(0, 2, stretch_turn, 0)

    def finish(a, half):
        cols = columns(a, half)
        part = acc[:, cols]
        total = part[HD:HD + 1, :]
        return part[:HD, :] * (1.0 / total), top[:, cols] + jnp.log2(total)

    def join(parts):
        peak = functools.reduce(jnp.maximum, [level for _, level in parts])
        shares = [jnp.exp2(level - peak) for _, level in parts]
        total = functools.reduce(jnp.add, shares)
        result = functools.reduce(
            jnp.add, [part.astype(jnp.float32) * (share / total) for (part, _), share in zip(parts, shares)]
        )
        return result, peak + jnp.log2(total)

    def arrived(n):
        for copy in o_copies(n):
            copy.wait_recv()
        return oget[n], lget[n]

    def send(n, result, level):
        osend[n] = result.astype(jnp.bfloat16)
        lsend[n] = level
        for copy in o_copies(n):
            copy.start()

    arrive(12, 13)
    turns(whole(28, 3), 4, {})
    for half in (0, 1):
        send(half, *finish(3, half))
    stretch_of(2)
    order = ((1, 1), (2, 0), (1, 0), (2, 1))
    score(*order[0], 24, 8, 0)
    for n, (a, half) in enumerate(order):
        if n + 1 < len(order):
            score(*order[n + 1], 24, 8, (n + 1) % 2)
        weigh(a, half, 24, 8, n % 2)
        if n == 1:
            send(3, *finish(1, 1))
            send(4, *finish(2, 0))
    send(2, *join([finish(1, 0), arrived(0)]))
    send(5, *join([finish(2, 1), arrived(1)]))
    turns(whole(12, 0), 4, {})
    turns(whole(16, 0) + whole(24, 0), 8, {})
    stretch_of(0)

    for d in range(1, HEADS):
        page_copy(d, (me - d + HEADS) % HEADS).wait_recv()
    own_pages().wait()
    for h in range(HEADS):
        paged[pl.ds(h, 4 * BLOCK, stride=HEADS), :] = landed[h].astype(jnp.float32)
    moved[...] = paged[...].astype(jnp.bfloat16)

    levels = []
    for half in (0, 1):
        result, level = join([finish(0, half), arrived((4, 3)[half])])
        acc[pl.ds(0, HD), columns(0, half)] = result
        levels.append(level)
    for half in (0, 1):
        result, _ = join([(acc[pl.ds(0, HD), columns(0, half)], levels[half]), arrived((2, 5)[half])])
        out[pl.ds(half * TILE, TILE), :] = result.T.astype(jnp.bfloat16)

    for m in range(MSGS):
        for forward in (True, False):
            kv_copy(m, forward).wait_send()
    for n in range(6):
        q_copy(n).wait_send()
    for hop in (1, 2, 3, 4):
        for forward in (True, False):
            st_copy(hop, forward, True).wait_send()

    @pl.when(z % NY != 0)
    def _():
        shift_copy().wait_send()

    for n in range(6):
        for copy in o_copies(n):
            copy.wait_send()
    for d in range(1, HEADS):
        page_copy(d, me).wait_send()


def body(queries, cache_kv, new_kv, cache_lengths, plan):
    smem = pl.BlockSpec(memory_space=pltpu.SMEM)
    hbm = pl.BlockSpec(memory_space=pltpu.HBM)
    out, moved = pl.pallas_call(
        kernel,
        out_shape=(
            jax.ShapeDtypeStruct((ROWS, HD), jnp.bfloat16),
            jax.ShapeDtypeStruct((4 * BLOCK * HEADS, HD), jnp.bfloat16),
        ),
        in_specs=[smem, smem, hbm, hbm, hbm],
        out_specs=(pl.BlockSpec(memory_space=pltpu.VMEM),) * 2,
        scratch_shapes=[
            pltpu.VMEM((PIECES, PIECE + HD, HD), jnp.bfloat16),
            pltpu.VMEM((NZ + 1, TOK + HD, HD), jnp.bfloat16),
            pltpu.VMEM((SUMS, PIECES * PIECE), jnp.bfloat16),
            pltpu.VMEM((NY * ROWS, HD), jnp.bfloat16),
            pltpu.VMEM((HD + SUMS, NY * ROWS), jnp.float32),
            pltpu.VMEM((1, NY * ROWS), jnp.float32),
            pltpu.VMEM((2, MOST * PIECE, TILE), jnp.float32),
            pltpu.VMEM((OWN, 2 * PIECE, HD), jnp.bfloat16),
            pltpu.VMEM((2 * TOK, HD), jnp.bfloat16),
            pltpu.VMEM((OWN + 1, 2 * PIECE, HD), jnp.float32),
            pltpu.VMEM((HEADS, 4 * BLOCK, HD), jnp.bfloat16),
            pltpu.VMEM((HEADS, 4 * BLOCK, HD), jnp.bfloat16),
            pltpu.VMEM((4 * BLOCK * HEADS, HD), jnp.float32),
            pltpu.VMEM((6, HD, TILE), jnp.bfloat16),
            pltpu.VMEM((6, 1, TILE), jnp.float32),
            pltpu.VMEM((6, HD, TILE), jnp.bfloat16),
            pltpu.VMEM((6, 1, TILE), jnp.float32),
            pltpu.SemaphoreType.DMA((OWN + 2,)),
            pltpu.SemaphoreType.DMA((PIECES,)),
            pltpu.SemaphoreType.DMA((PIECES,)),
            pltpu.SemaphoreType.DMA((4, 2)),
            pltpu.SemaphoreType.DMA((4, 2)),
            pltpu.SemaphoreType.DMA,
            pltpu.SemaphoreType.DMA,
            pltpu.SemaphoreType.DMA((6,)),
            pltpu.SemaphoreType.DMA((6,)),
            pltpu.SemaphoreType.DMA((6,)),
            pltpu.SemaphoreType.DMA((6,)),
            pltpu.SemaphoreType.DMA((6,)),
            pltpu.SemaphoreType.DMA((6,)),
            pltpu.SemaphoreType.DMA((HEADS,)),
            pltpu.SemaphoreType.DMA((HEADS,)),
            pltpu.SemaphoreType.DMA,
        ],
        compiler_params=pltpu.CompilerParams(
            collective_id=0, has_side_effects=True, vmem_limit_bytes=32 * 2 ** 20
        ),
        name="stretch_attention",
    )(
        *(pltpu.with_memory_space_constraint(x, pltpu.HBM) for x in (
            cache_lengths,
            plan.reshape(PAGES),
            queries.reshape(ROWS, HD),
            cache_kv.reshape(2 * CACHE, HD),
            new_kv.reshape(2 * TOK, HD),
        )),
    )
    attended = out.reshape(TOK, 1, GROUP, HD)
    migrated = moved.reshape(1, 1, 2, BLOCK, 2, HEADS, HD)
    return attended, migrated


def solution(mesh):
    return jax.shard_map(
        body,
        mesh=mesh,
        in_specs=(
            P("ctx", ("head", "inst"), None, None),
            P("ctx", None, ("head", "inst"), None),
            P("ctx", None, ("head", "inst"), None),
            P(),
            P("ctx", None),
        ),
        out_specs=(
            P("ctx", ("head", "inst"), None, None),
            P("inst", "ctx", "head", None, None, None, None),
        ),
        check_vma=False,
    )
```

```python
import functools
import math

import jax
import jax.numpy as jnp
from jax import lax
from jax.experimental import pallas as pl
from jax.experimental.pallas import tpu as pltpu
from jax.sharding import PartitionSpec as P

MESH = pl.DeviceIdType.MESH
NY, NZ = 4, 8
NH, NI = 2, 4
HEADS = NH * NI
HD = 128
GROUP = 8
TOK = 128
ROWS = TOK * GROUP
CACHE = 512
PIECE = 128
OWN = CACHE // PIECE
MSGS = 14
PIECES = OWN + 2 * MSGS
MOST = 8
TILE = 512
BLOCK = 16
PAGES = TOK // BLOCK
CAP = PAGES // 2
SUMS = 16
SCALE = HD ** -0.5 * math.log2(math.e)
LOWEST = -1.0e30
NT = (((1,), (1,)), ((), ()))
OFFSETS = (0, 1, 3, 2)


def piece_of(m, forward):
    return OWN + 2 * m + (0 if forward else 1)


def quarter_of(m, forward):
    return (m + (0 if forward else 2)) % OWN


def shard_of(m, forward):
    hop = 1 + m // OWN
    return (-hop if forward else hop), quarter_of(m, forward)


def kernel(lens, plan, q_in, cache_in, fresh_in, out, moved,
           kv, st, live, qs, acc, top, sbuf, raw, fraw, wide, packed, landed, paged, osend, lsend, oget, lget,
           in_s, kv_s, kv_r, st_s, st_r, sh_s, sh_r, q_s, q_r, o_s, o_r, l_s, l_r, mg_s, mg_r, own_s):
    ctx = lax.axis_index("ctx")
    head = lax.axis_index("head")
    inst = lax.axis_index("inst")
    y, z = ctx // NZ, ctx % NZ
    me = head * NI + inst

    def at_z(d):
        return (y * NZ + (z + d + NZ) % NZ, head, inst)

    def at_y(d):
        return (((y + d + NY) % NY) * NZ + z, head, inst)

    def at_head(h):
        return (ctx, h // NI, h % NI)

    loads = [
        pltpu.make_async_copy(cache_in.at[pl.ds(n * 2 * PIECE, 2 * PIECE)], raw.at[n], in_s.at[n])
        for n in range(OWN)
    ]
    loads.append(pltpu.make_async_copy(fresh_in, fraw, in_s.at[OWN]))
    loads.append(pltpu.make_async_copy(q_in, qs.at[pl.ds(0, ROWS)], in_s.at[OWN + 1]))
    loads[0].start()

    barrier = pltpu.get_barrier_semaphore()
    peers = [at_z(1), at_z(-1), at_y(1), at_y(2), at_y(3)]
    peers += [at_head((me + d) % HEADS) for d in range(1, HEADS)]
    for peer in peers:
        pl.semaphore_signal(barrier, inc=1, device_id=peer, device_id_type=MESH)
    for n in (OWN, 2, 1, 3, OWN + 1):
        loads[n].start()

    def kv_copy(m, forward):
        src = quarter_of(m, forward) if m < OWN else piece_of(m - OWN, forward)
        dst = piece_of(m, forward)
        return pltpu.make_async_remote_copy(
            src_ref=kv.at[src],
            dst_ref=kv.at[dst],
            send_sem=kv_s.at[dst],
            recv_sem=kv_r.at[dst],
            device_id=at_z(1 if forward else -1),
            device_id_type=MESH,
        )

    def arrive(*messages):
        for m in messages:
            for forward in (True, False):
                kv_copy(m, forward).wait_recv()

    def pass_on(*messages):
        for m in messages:
            for forward in (True, False):
                kv_copy(m + OWN, forward).start()

    def q_copy(n):
        half = (0, 1, 0, 1, 0, 1)[n]
        src = (0, 0, 0, 0, 2, 1)[n]
        dst = (2, 2, 1, 1, 3, 3)[n]
        to = (1, 1, -1, -1, 1, -1)[n]
        if n < 4:
            src_ref = q_in.at[pl.ds(half * TILE, TILE)]
        else:
            src_ref = qs.at[pl.ds(src * ROWS + half * TILE, TILE)]
        return pltpu.make_async_remote_copy(
            src_ref=src_ref,
            dst_ref=qs.at[pl.ds(dst * ROWS + half * TILE, TILE)],
            send_sem=q_s.at[n],
            recv_sem=q_r.at[n],
            device_id=at_y(to),
            device_id_type=MESH,
        )

    def place(zz):
        zz = (zz + NZ) % NZ
        return (zz % NY) * 2 + zz // NY

    def shift_copy():
        return pltpu.make_async_remote_copy(
            src_ref=st.at[NZ],
            dst_ref=st.at[place(z)],
            send_sem=sh_s,
            recv_sem=sh_r,
            device_id=(((y - z + NZ) % NY) * NZ + z, head, inst),
            device_id_type=MESH,
        )

    def stay_copy():
        return pltpu.make_async_copy(st.at[NZ], st.at[place(z)], sh_r)

    def st_ref(zz, hop, forward):
        if hop < 4:
            return st.at[place(zz)]
        return st.at[place(zz), pl.ds(0 if forward else TOK, TOK)]

    def st_copy(hop, forward, sending):
        sign = 1 if forward else -1
        ref = st_ref(z - sign * (hop - 1 if sending else hop), hop, forward)
        return pltpu.make_async_remote_copy(
            src_ref=ref,
            dst_ref=ref,
            send_sem=st_s.at[hop - 1, int(forward)],
            recv_sem=st_r.at[hop - 1, int(forward)],
            device_id=at_z(sign),
            device_id_type=MESH,
        )

    def next_stretch(hop):
        for forward in (True, False):
            st_copy(hop, forward, False).wait_recv()
            if hop < 4:
                st_copy(hop + 1, forward, True).start()

    def page_copy(d, dst):
        to = (me + d) % HEADS
        return pltpu.make_async_remote_copy(
            src_ref=packed.at[(to % NI) * NH + to // NI],
            dst_ref=landed.at[dst],
            send_sem=mg_s.at[d],
            recv_sem=mg_r.at[d],
            device_id=at_head(to),
            device_id_type=MESH,
        )

    def own_pages():
        return pltpu.make_async_copy(packed.at[inst * NH + head], landed.at[me], own_s)

    def o_copies(n):
        to = at_y((1, -1, 1, 1, -1, -1)[n])
        return (
            pltpu.make_async_remote_copy(
                src_ref=osend.at[n], dst_ref=oget.at[n], send_sem=o_s.at[n], recv_sem=o_r.at[n],
                device_id=to, device_id_type=MESH,
            ),
            pltpu.make_async_remote_copy(
                src_ref=lsend.at[n], dst_ref=lget.at[n], send_sem=l_s.at[n], recv_sem=l_r.at[n],
                device_id=to, device_id_type=MESH,
            ),
        )

    length = lens[ctx]

    def split(n):
        return wide[n, pl.ds(0, PIECE, stride=2), :], wide[n, pl.ds(1, PIECE, stride=2), :]

    def own_piece(n, first):
        loads[n].wait()
        wide[n] = raw[n].astype(jnp.float32)
        keys, values = split(n)
        first = keys[0:1, :] if n == 0 else first
        usable = lax.broadcasted_iota(jnp.int32, (PIECE, HD), 0) + n * PIECE < length
        kv[n, pl.ds(0, PIECE), :] = jnp.where(usable, keys, jnp.broadcast_to(first, (PIECE, HD))).astype(jnp.bfloat16)
        kv[n, pl.ds(PIECE, HD), :] = jnp.where(usable, values, 0.0).T.astype(jnp.bfloat16)
        return first

    first = own_piece(0, None)
    pl.semaphore_wait(barrier, len(peers))
    kv_copy(0, True).start()
    loads[OWN].wait()
    fresh = fraw[...].astype(jnp.float32)
    wide[OWN] = fresh
    keys, values = split(OWN)
    st[NZ, pl.ds(0, TOK), :] = keys.astype(jnp.bfloat16)
    st[NZ, pl.ds(TOK, HD), :] = values.T.astype(jnp.bfloat16)

    @pl.when(z % NY != 0)
    def _():
        shift_copy().start()

    @pl.when(z % NY == 0)
    def _():
        stay_copy().start()

    for n in (0, 2, 1, 3):
        q_copy(n).start()
    own_piece(2, first)
    kv_copy(0, False).start()
    own_piece(1, first)
    kv_copy(1, True).start()
    own_piece(3, first)
    kv_copy(1, False).start()
    for forward in (True, False):
        kv_copy(2, forward).start()

    def empty(n, carry):
        acc[:, pl.ds(pl.multiple_of(n * TILE, TILE), TILE)] = jnp.zeros((HD + SUMS, TILE), jnp.float32)
        return carry

    lax.fori_loop(0, NY * ROWS // TILE, empty, 0)
    top[...] = jnp.full((1, NY * ROWS), LOWEST, jnp.float32)
    origin = {n: (0, n) for n in range(OWN)}
    for m in range(MSGS):
        for forward in (True, False):
            origin[piece_of(m, forward)] = shard_of(m, forward)
    lane = lax.broadcasted_iota(jnp.int32, (SUMS, PIECE), 1)
    for n in range(PIECES):
        d, quarter = origin[n]
        filled = lens[y * NZ + (z + d + NZ) % NZ]
        live[:, pl.ds(n * PIECE, PIECE)] = jnp.where(lane + quarter * PIECE < filled, 1.0, 0.0).astype(jnp.bfloat16)

    targets = []
    for b in range(PAGES):
        earlier = jnp.int32(0)
        for a in range(b):
            earlier = earlier + (plan[a] == plan[b]).astype(jnp.int32)
        targets.append(plan[b] * CAP + earlier)
    for t in range(NI * CAP):
        page = jnp.zeros((2 * BLOCK, HD), jnp.float32)
        for b in range(PAGES):
            page = page + fresh[2 * BLOCK * b:2 * BLOCK * (b + 1), :] * (targets[b] == t).astype(jnp.float32)
        packed[t // 2, pl.ds((t % 2) * 2 * BLOCK, 2 * BLOCK), :] = page.astype(jnp.bfloat16)
    for d in range(1, HEADS):
        page_copy(d, me).start()
    own_pages().start()

    @pl.when(z % NY != 0)
    def _():
        shift_copy().wait_recv()

    @pl.when(z % NY == 0)
    def _():
        stay_copy().wait()

    for forward in (True, False):
        st_copy(1, forward, True).start()
    for forward in (True, False):
        kv_copy(3, forward).start()

    def columns(a, half):
        return pl.ds(pl.multiple_of(a * ROWS + half * TILE, TILE), TILE)

    def add(cols, scores, vals):
        before = top[:, cols]
        peak = jnp.maximum(before, jnp.max(scores, axis=0, keepdims=True) * SCALE)
        weights = jnp.exp2(scores * SCALE - peak).astype(jnp.bfloat16)
        part = jnp.dot(vals, weights, preferred_element_type=jnp.float32)
        acc[:, cols] = acc[:, cols] * jnp.exp2(before - peak) + part
        top[:, cols] = peak

    def score(a, half, start, count, slot):
        keys = kv[pl.ds(start, count), pl.ds(0, PIECE), :].reshape(count * PIECE, HD)
        sbuf[slot, pl.ds(0, count * PIECE), :] = lax.dot_general(
            keys, qs[columns(a, half), :], NT, preferred_element_type=jnp.float32
        )

    def weigh(a, half, start, count, slot):
        vals = jnp.concatenate([kv[start + n, pl.ds(PIECE, HD), :] for n in range(count)], axis=1)
        sums = live[:, pl.ds(pl.multiple_of(start * PIECE, PIECE), count * PIECE)]
        scores = sbuf[slot, pl.ds(0, count * PIECE), :]
        add(columns(a, half), scores, jnp.concatenate([vals, sums], axis=0))

    first_turns = (
        ((0, 0, 0), (0, 1, 0)),
        ((1, 0, 0), (2, 0, 0)),
        ((1, 1, 0), (2, 1, 0)),
    )
    more_turns = (
        ((1, 0, 8), (1, 1, 8)),
        ((2, 0, 8), (2, 1, 8)),
        ((3, 0, 0), (3, 1, 0)),
        ((3, 0, 8), (3, 1, 8)),
    )
    def whole(start, *shards):
        return tuple(((a, 0, start), (a, 1, start)) for a in shards)

    def event_0():
        q_copy(2).wait_recv()

    def event_1():
        q_copy(0).wait_recv()
        q_copy(4).start()
        next_stretch(1)
        arrive(2)
        pass_on(2)
        q_copy(3).wait_recv()
        q_copy(5).start()
        q_copy(1).wait_recv()
        arrive(3)
        pass_on(3)

    def event_4():
        next_stretch(2)
        pass_on(4, 5)
        q_copy(4).wait_recv()
        q_copy(5).wait_recv()

    def turns(table, count, events):
        def tile(n, u):
            found = [jnp.int32(value) for value in table[0][u]]
            for when in range(1, len(table)):
                found = [jnp.where(n == when, value, old) for value, old in zip(table[when][u], found)]
            return found

        def one_turn(n, carry):
            for when, event in events.items():
                pl.when(n == when)(event)
            one, two, after = tile(n, 0), tile(n, 1), tile(n + 1, 0)
            score(*two, count, 1)
            weigh(*one, count, 0)
            score(*after, count, 0)
            weigh(*two, count, 1)
            return carry

        score(*table[0][0], count, 0)
        lax.fori_loop(0, len(table) - 1, one_turn, 0)
        one, two = table[-1]
        score(*two, count, 1)
        weigh(*one, count, 0)
        weigh(*two, count, 1)

    arrive(0, 1)
    pass_on(0, 1)
    loads[OWN + 1].wait()
    turns(first_turns, 8, {0: event_0, 1: event_1})
    turns(whole(8, 0), 4, {})
    arrive(4, 5)
    turns(more_turns, 8, {1: event_4})
    arrive(6, 7)

    def event_third():
        next_stretch(3)
        pass_on(6, 7)

    turns(whole(16, 3, 1, 2), 4, {1: event_third})
    arrive(8, 9)
    pass_on(8, 9)
    turns(whole(20, 3, 1, 2), 4, {})

    def stretch(a, row):
        pairs = [(j - y + NY) % NY for j in range(row + 1)]
        keys = jnp.concatenate([st[pl.ds(2 * k, 2), pl.ds(0, TOK), :].reshape(2 * TOK, HD) for k in pairs], axis=0)
        vals = jnp.concatenate([st[2 * k + n, pl.ds(TOK, HD), :] for k in pairs for n in (0, 1)], axis=1)
        vals = jnp.concatenate([vals, jnp.ones((SUMS, 2 * TOK * (row + 1)), jnp.bfloat16)], axis=0)
        key = lax.broadcasted_iota(jnp.int32, (2 * TOK, TILE), 0)
        token = lax.broadcasted_iota(jnp.int32, (2 * TOK, TILE), 1) // GROUP
        key_pos = pairs[row] * TOK + key + jnp.where(key >= TOK, NY * TOK - TOK, 0)
        scored = []
        for half in (0, 1):
            s = lax.dot_general(keys, qs[columns(a, half), :], NT, preferred_element_type=jnp.float32)
            usable = key_pos <= z * TOK + half * (TILE // GROUP) + token
            own = jnp.where(usable, s[row * 2 * TOK:, :], LOWEST)
            scored.append(own if row == 0 else jnp.concatenate([s[:row * 2 * TOK, :], own], axis=0))
        for half in (0, 1):
            add(columns(a, half), scored[half], vals)

    def stretch_of(a):
        offset = jnp.where(a == 3, 2, jnp.where(a == 2, 3, a))
        mine_row = (y + offset) % NY
        for row in range(NY):
            pl.when(mine_row == row)(functools.partial(stretch, a, row))

    next_stretch(4)

    def third_step():
        arrive(10, 11)
        turns(whole(24, 3), 4, {})

    def stretch_turn(n, carry):
        pl.when(n == 1)(third_step)
        stretch_of(jnp.where(n == 0, 3, 1))
        return carry

    lax.fori_loop(0, 2, stretch_turn, 0)

    def finish(a, half):
        cols = columns(a, half)
        part = acc[:, cols]
        total = part[HD:HD + 1, :]
        return part[:HD, :] * (1.0 / total), top[:, cols] + jnp.log2(total)

    def join(parts):
        peak = functools.reduce(jnp.maximum, [level for _, level in parts])
        shares = [jnp.exp2(level - peak) for _, level in parts]
        total = functools.reduce(jnp.add, shares)
        result = functools.reduce(
            jnp.add, [part.astype(jnp.float32) * (share / total) for (part, _), share in zip(parts, shares)]
        )
        return result, peak + jnp.log2(total)

    def arrived(n):
        for copy in o_copies(n):
            copy.wait_recv()
        return oget[n], lget[n]

    def send(n, result, level):
        osend[n] = result.astype(jnp.bfloat16)
        lsend[n] = level
        for copy in o_copies(n):
            copy.start()

    arrive(12, 13)
    turns(whole(28, 3), 4, {})
    for half in (0, 1):
        send(half, *finish(3, half))
    stretch_of(2)
    order = ((1, 1), (2, 0), (1, 0), (2, 1))
    score(*order[0], 24, 8, 0)
    for n, (a, half) in enumerate(order):
        if n + 1 < len(order):
            score(*order[n + 1], 24, 8, (n + 1) % 2)
        weigh(a, half, 24, 8, n % 2)
        if n == 1:
            send(3, *finish(1, 1))
            send(4, *finish(2, 0))
    send(2, *join([finish(1, 0), arrived(0)]))
    send(5, *join([finish(2, 1), arrived(1)]))
    turns(whole(12, 0), 4, {})
    turns(whole(16, 0) + whole(24, 0), 8, {})
    stretch_of(0)

    for d in range(1, HEADS):
        page_copy(d, (me - d + HEADS) % HEADS).wait_recv()
    own_pages().wait()
    for h in range(HEADS):
        paged[pl.ds(h, 4 * BLOCK, stride=HEADS), :] = landed[h].astype(jnp.float32)
    moved[...] = paged[...].astype(jnp.bfloat16)

    levels = []
    for half in (0, 1):
        result, level = join([finish(0, half), arrived((4, 3)[half])])
        acc[pl.ds(0, HD), columns(0, half)] = result
        levels.append(level)
    for half in (0, 1):
        result, _ = join([(acc[pl.ds(0, HD), columns(0, half)], levels[half]), arrived((2, 5)[half])])
        out[pl.ds(half * TILE, TILE), :] = result.T.astype(jnp.bfloat16)

    for m in range(MSGS):
        for forward in (True, False):
            kv_copy(m, forward).wait_send()
    for n in range(6):
        q_copy(n).wait_send()
    for hop in (1, 2, 3, 4):
        for forward in (True, False):
            st_copy(hop, forward, True).wait_send()

    @pl.when(z % NY != 0)
    def _():
        shift_copy().wait_send()

    for n in range(6):
        for copy in o_copies(n):
            copy.wait_send()
    for d in range(1, HEADS):
        page_copy(d, me).wait_send()


def write(out_in, moved_in, out, moved, sems):
    copies = [
        pltpu.make_async_copy(out_in.at[pl.ds(n * 256, 256)], out.at[pl.ds(n * 256, 256)], sems.at[n]) for n in range(4)
    ]
    copies += [
        pltpu.make_async_copy(moved_in.at[pl.ds(n * 256, 256)], moved.at[pl.ds(n * 256, 256)], sems.at[4 + n])
        for n in range(2)
    ]
    for copy in copies:
        copy.start()
    for copy in copies:
        copy.wait()


def body(queries, cache_kv, new_kv, cache_lengths, plan):
    smem = pl.BlockSpec(memory_space=pltpu.SMEM)
    hbm = pl.BlockSpec(memory_space=pltpu.HBM)
    out, moved = pl.pallas_call(
        kernel,
        out_shape=(
            jax.ShapeDtypeStruct((ROWS, HD), jnp.bfloat16),
            jax.ShapeDtypeStruct((4 * BLOCK * HEADS, HD), jnp.bfloat16),
        ),
        in_specs=[smem, smem, hbm, hbm, hbm],
        out_specs=(pl.BlockSpec(memory_space=pltpu.VMEM),) * 2,
        scratch_shapes=[
            pltpu.VMEM((PIECES, PIECE + HD, HD), jnp.bfloat16),
            pltpu.VMEM((NZ + 1, TOK + HD, HD), jnp.bfloat16),
            pltpu.VMEM((SUMS, PIECES * PIECE), jnp.bfloat16),
            pltpu.VMEM((NY * ROWS, HD), jnp.bfloat16),
            pltpu.VMEM((HD + SUMS, NY * ROWS), jnp.float32),
            pltpu.VMEM((1, NY * ROWS), jnp.float32),
            pltpu.VMEM((2, MOST * PIECE, TILE), jnp.float32),
            pltpu.VMEM((OWN, 2 * PIECE, HD), jnp.bfloat16),
            pltpu.VMEM((2 * TOK, HD), jnp.bfloat16),
            pltpu.VMEM((OWN + 1, 2 * PIECE, HD), jnp.float32),
            pltpu.VMEM((HEADS, 4 * BLOCK, HD), jnp.bfloat16),
            pltpu.VMEM((HEADS, 4 * BLOCK, HD), jnp.bfloat16),
            pltpu.VMEM((4 * BLOCK * HEADS, HD), jnp.float32),
            pltpu.VMEM((6, HD, TILE), jnp.bfloat16),
            pltpu.VMEM((6, 1, TILE), jnp.float32),
            pltpu.VMEM((6, HD, TILE), jnp.bfloat16),
            pltpu.VMEM((6, 1, TILE), jnp.float32),
            pltpu.SemaphoreType.DMA((OWN + 2,)),
            pltpu.SemaphoreType.DMA((PIECES,)),
            pltpu.SemaphoreType.DMA((PIECES,)),
            pltpu.SemaphoreType.DMA((4, 2)),
            pltpu.SemaphoreType.DMA((4, 2)),
            pltpu.SemaphoreType.DMA,
            pltpu.SemaphoreType.DMA,
            pltpu.SemaphoreType.DMA((6,)),
            pltpu.SemaphoreType.DMA((6,)),
            pltpu.SemaphoreType.DMA((6,)),
            pltpu.SemaphoreType.DMA((6,)),
            pltpu.SemaphoreType.DMA((6,)),
            pltpu.SemaphoreType.DMA((6,)),
            pltpu.SemaphoreType.DMA((HEADS,)),
            pltpu.SemaphoreType.DMA((HEADS,)),
            pltpu.SemaphoreType.DMA,
        ],
        compiler_params=pltpu.CompilerParams(
            collective_id=0, has_side_effects=True, vmem_limit_bytes=32 * 2 ** 20
        ),
        name="stretch_attention",
    )(
        *(pltpu.with_memory_space_constraint(x, pltpu.HBM) for x in (
            cache_lengths,
            plan.reshape(PAGES),
            queries.reshape(ROWS, HD),
            cache_kv.reshape(2 * CACHE, HD),
            new_kv.reshape(2 * TOK, HD),
        )),
    )
    vmem = pl.BlockSpec(memory_space=pltpu.VMEM)
    out, moved = pl.pallas_call(
        write,
        out_shape=(
            jax.ShapeDtypeStruct((ROWS, HD), jnp.bfloat16),
            jax.ShapeDtypeStruct((4 * BLOCK * HEADS, HD), jnp.bfloat16),
        ),
        in_specs=[vmem, vmem],
        out_specs=(hbm, hbm),
        scratch_shapes=[pltpu.SemaphoreType.DMA((6,))],
        name="write_results",
    )(*(pltpu.with_memory_space_constraint(x, pltpu.VMEM) for x in (out, moved)))
    attended = out.reshape(TOK, 1, GROUP, HD)
    migrated = moved.reshape(1, 1, 2, BLOCK, 2, HEADS, HD)
    return attended, migrated


def solution(mesh):
    return jax.shard_map(
        body,
        mesh=mesh,
        in_specs=(
            P("ctx", ("head", "inst"), None, None),
            P("ctx", None, ("head", "inst"), None),
            P("ctx", None, ("head", "inst"), None),
            P(),
            P("ctx", None),
        ),
        out_specs=(
            P("ctx", ("head", "inst"), None, None),
            P("inst", "ctx", "head", None, None, None, None),
        ),
        check_vma=False,
    )
```

```python
import functools
import math

import jax
import jax.numpy as jnp
from jax import lax
from jax.experimental import pallas as pl
from jax.experimental.pallas import tpu as pltpu
from jax.sharding import PartitionSpec as P

MESH = pl.DeviceIdType.MESH
NY, NZ = 4, 8
NH, NI = 2, 4
HEADS = NH * NI
HD = 128
GROUP = 8
TOK = 128
ROWS = TOK * GROUP
CACHE = 512
PIECE = 128
OWN = CACHE // PIECE
MSGS = 14
PIECES = OWN + 2 * MSGS
MOST = 8
TILE = 512
BLOCK = 16
PAGES = TOK // BLOCK
CAP = PAGES // 2
SUMS = 16
SCALE = HD ** -0.5 * math.log2(math.e)
LOWEST = -1.0e30
NT = (((1,), (1,)), ((), ()))
OFFSETS = (0, 1, 3, 2)


def piece_of(m, forward):
    return OWN + 2 * m + (0 if forward else 1)


def quarter_of(m, forward):
    return (m + (0 if forward else 2)) % OWN


def shard_of(m, forward):
    hop = 1 + m // OWN
    return (-hop if forward else hop), quarter_of(m, forward)


def kernel(lens, plan, q_in, cache_in, fresh_in, out, moved,
           kv, st, live, qs, acc, top, sbuf, raw, fraw, wide, packed, landed, paged, osend, lsend, oget, lget,
           in_s, kv_s, kv_r, st_s, st_r, sh_s, sh_r, q_s, q_r, o_s, o_r, l_s, l_r, mg_s, mg_r, own_s):
    ctx = lax.axis_index("ctx")
    head = lax.axis_index("head")
    inst = lax.axis_index("inst")
    y, z = ctx // NZ, ctx % NZ
    me = head * NI + inst

    def at_z(d):
        return (y * NZ + (z + d + NZ) % NZ, head, inst)

    def at_y(d):
        return (((y + d + NY) % NY) * NZ + z, head, inst)

    def at_head(h):
        return (ctx, h // NI, h % NI)

    loads = [
        pltpu.make_async_copy(cache_in.at[pl.ds(n * 2 * PIECE, 2 * PIECE)], raw.at[n], in_s.at[n])
        for n in range(OWN)
    ]
    loads.append(pltpu.make_async_copy(fresh_in, fraw, in_s.at[OWN]))
    loads.append(pltpu.make_async_copy(q_in, qs.at[pl.ds(0, ROWS)], in_s.at[OWN + 1]))
    loads[0].start()

    barrier = pltpu.get_barrier_semaphore()
    peers = [at_z(1), at_z(-1), at_y(1), at_y(2), at_y(3)]
    peers += [at_head((me + d) % HEADS) for d in range(1, HEADS)]
    for peer in peers:
        pl.semaphore_signal(barrier, inc=1, device_id=peer, device_id_type=MESH)
    for n in (OWN, 2, 1, 3, OWN + 1):
        loads[n].start()

    def kv_copy(m, forward):
        src = quarter_of(m, forward) if m < OWN else piece_of(m - OWN, forward)
        dst = piece_of(m, forward)
        return pltpu.make_async_remote_copy(
            src_ref=kv.at[src],
            dst_ref=kv.at[dst],
            send_sem=kv_s.at[dst],
            recv_sem=kv_r.at[dst],
            device_id=at_z(1 if forward else -1),
            device_id_type=MESH,
        )

    def arrive(*messages):
        for m in messages:
            for forward in (True, False):
                kv_copy(m, forward).wait_recv()

    def pass_on(*messages):
        for m in messages:
            for forward in (True, False):
                kv_copy(m + OWN, forward).start()

    def q_copy(n):
        half = (0, 1, 0, 1, 0, 1)[n]
        src = (0, 0, 0, 0, 2, 1)[n]
        dst = (2, 2, 1, 1, 3, 3)[n]
        to = (1, 1, -1, -1, 1, -1)[n]
        if n < 4:
            src_ref = q_in.at[pl.ds(half * TILE, TILE)]
        else:
            src_ref = qs.at[pl.ds(src * ROWS + half * TILE, TILE)]
        return pltpu.make_async_remote_copy(
            src_ref=src_ref,
            dst_ref=qs.at[pl.ds(dst * ROWS + half * TILE, TILE)],
            send_sem=q_s.at[n],
            recv_sem=q_r.at[n],
            device_id=at_y(to),
            device_id_type=MESH,
        )

    def place(zz):
        zz = (zz + NZ) % NZ
        return (zz % NY) * 2 + zz // NY

    def shift_copy():
        return pltpu.make_async_remote_copy(
            src_ref=st.at[NZ],
            dst_ref=st.at[place(z)],
            send_sem=sh_s,
            recv_sem=sh_r,
            device_id=(((y - z + NZ) % NY) * NZ + z, head, inst),
            device_id_type=MESH,
        )

    def stay_copy():
        return pltpu.make_async_copy(st.at[NZ], st.at[place(z)], sh_r)

    def st_ref(zz, hop, forward):
        if hop < 4:
            return st.at[place(zz)]
        return st.at[place(zz), pl.ds(0 if forward else TOK, TOK)]

    def st_copy(hop, forward, sending):
        sign = 1 if forward else -1
        ref = st_ref(z - sign * (hop - 1 if sending else hop), hop, forward)
        return pltpu.make_async_remote_copy(
            src_ref=ref,
            dst_ref=ref,
            send_sem=st_s.at[hop - 1, int(forward)],
            recv_sem=st_r.at[hop - 1, int(forward)],
            device_id=at_z(sign),
            device_id_type=MESH,
        )

    def next_stretch(hop):
        for forward in (True, False):
            st_copy(hop, forward, False).wait_recv()
            if hop < 4:
                st_copy(hop + 1, forward, True).start()

    def page_copy(d, dst):
        to = (me + d) % HEADS
        return pltpu.make_async_remote_copy(
            src_ref=packed.at[(to % NI) * NH + to // NI],
            dst_ref=landed.at[dst],
            send_sem=mg_s.at[d],
            recv_sem=mg_r.at[d],
            device_id=at_head(to),
            device_id_type=MESH,
        )

    def own_pages():
        return pltpu.make_async_copy(packed.at[inst * NH + head], landed.at[me], own_s)

    def o_copies(n):
        to = at_y((1, -1, 1, 1, -1, -1)[n])
        return (
            pltpu.make_async_remote_copy(
                src_ref=osend.at[n], dst_ref=oget.at[n], send_sem=o_s.at[n], recv_sem=o_r.at[n],
                device_id=to, device_id_type=MESH,
            ),
            pltpu.make_async_remote_copy(
                src_ref=lsend.at[n], dst_ref=lget.at[n], send_sem=l_s.at[n], recv_sem=l_r.at[n],
                device_id=to, device_id_type=MESH,
            ),
        )

    length = lens[ctx]

    def split(n):
        return wide[n, pl.ds(0, PIECE, stride=2), :], wide[n, pl.ds(1, PIECE, stride=2), :]

    def own_piece(n, first):
        loads[n].wait()
        wide[n, pl.ds(0, 2 * PIECE), :] = raw[n].astype(jnp.float32)
        keys, values = split(n)
        first = keys[0:1, :] if n == 0 else first
        usable = lax.broadcasted_iota(jnp.int32, (PIECE, HD), 0) + n * PIECE < length
        kv[n, pl.ds(0, PIECE), :] = jnp.where(usable, keys, jnp.broadcast_to(first, (PIECE, HD))).astype(jnp.bfloat16)
        kv[n, pl.ds(PIECE, HD), :] = jnp.where(usable, values, 0.0).T.astype(jnp.bfloat16)
        return first

    first = own_piece(0, None)
    pl.semaphore_wait(barrier, len(peers))
    kv_copy(0, True).start()
    loads[OWN].wait()
    fresh = fraw[...].astype(jnp.float32)
    wide[OWN, pl.ds(0, 2 * TOK), :] = fresh
    keys, values = split(OWN)
    st[NZ, pl.ds(0, TOK), :] = keys.astype(jnp.bfloat16)
    st[NZ, pl.ds(TOK, HD), :] = values.T.astype(jnp.bfloat16)

    @pl.when(z % NY != 0)
    def _():
        shift_copy().start()

    @pl.when(z % NY == 0)
    def _():
        stay_copy().start()

    for n in (0, 2, 1, 3):
        q_copy(n).start()
    own_piece(2, first)
    kv_copy(0, False).start()
    own_piece(1, first)
    kv_copy(1, True).start()
    own_piece(3, first)
    kv_copy(1, False).start()
    for forward in (True, False):
        kv_copy(2, forward).start()

    def empty(n, carry):
        acc[:, pl.ds(pl.multiple_of(n * TILE, TILE), TILE)] = jnp.zeros((HD + SUMS, TILE), jnp.float32)
        return carry

    lax.fori_loop(0, NY * ROWS // TILE, empty, 0)
    top[...] = jnp.full((1, NY * ROWS), LOWEST, jnp.float32)
    origin = {n: (0, n) for n in range(OWN)}
    for m in range(MSGS):
        for forward in (True, False):
            origin[piece_of(m, forward)] = shard_of(m, forward)
    lane = lax.broadcasted_iota(jnp.int32, (SUMS, PIECE), 1)
    for n in range(PIECES):
        d, quarter = origin[n]
        filled = lens[y * NZ + (z + d + NZ) % NZ]
        live[:, pl.ds(n * PIECE, PIECE)] = jnp.where(lane + quarter * PIECE < filled, 1.0, 0.0).astype(jnp.bfloat16)

    targets = []
    for b in range(PAGES):
        earlier = jnp.int32(0)
        for a in range(b):
            earlier = earlier + (plan[a] == plan[b]).astype(jnp.int32)
        targets.append(plan[b] * CAP + earlier)
    for t in range(NI * CAP):
        page = jnp.zeros((2 * BLOCK, HD), jnp.float32)
        for b in range(PAGES):
            page = page + fresh[2 * BLOCK * b:2 * BLOCK * (b + 1), :] * (targets[b] == t).astype(jnp.float32)
        packed[t // 2, pl.ds((t % 2) * 2 * BLOCK, 2 * BLOCK), :] = page.astype(jnp.bfloat16)
    for d in range(1, HEADS):
        page_copy(d, me).start()
    own_pages().start()

    @pl.when(z % NY != 0)
    def _():
        shift_copy().wait_recv()

    @pl.when(z % NY == 0)
    def _():
        stay_copy().wait()

    for forward in (True, False):
        st_copy(1, forward, True).start()
    for forward in (True, False):
        kv_copy(3, forward).start()

    def columns(a, half):
        return pl.ds(pl.multiple_of(a * ROWS + half * TILE, TILE), TILE)

    def add(cols, scores, vals):
        before = top[:, cols]
        peak = jnp.maximum(before, jnp.max(scores, axis=0, keepdims=True) * SCALE)
        weights = jnp.exp2(scores * SCALE - peak).astype(jnp.bfloat16)
        part = jnp.dot(vals, weights, preferred_element_type=jnp.float32)
        acc[:, cols] = acc[:, cols] * jnp.exp2(before - peak) + part
        top[:, cols] = peak

    def score(a, half, start, count, slot):
        keys = kv[pl.ds(start, count), pl.ds(0, PIECE), :].reshape(count * PIECE, HD)
        sbuf[slot, pl.ds(0, count * PIECE), :] = lax.dot_general(
            keys, qs[columns(a, half), :], NT, preferred_element_type=jnp.float32
        )

    def weigh(a, half, start, count, slot):
        vals = jnp.concatenate([kv[start + n, pl.ds(PIECE, HD), :] for n in range(count)], axis=1)
        sums = live[:, pl.ds(pl.multiple_of(start * PIECE, PIECE), count * PIECE)]
        scores = sbuf[slot, pl.ds(0, count * PIECE), :]
        add(columns(a, half), scores, jnp.concatenate([vals, sums], axis=0))

    first_turns = (
        ((0, 0, 0), (0, 1, 0)),
        ((1, 0, 0), (2, 0, 0)),
        ((1, 1, 0), (2, 1, 0)),
    )
    more_turns = (
        ((1, 0, 8), (1, 1, 8)),
        ((2, 0, 8), (2, 1, 8)),
        ((3, 0, 0), (3, 1, 0)),
        ((3, 0, 8), (3, 1, 8)),
    )
    def whole(start, *shards):
        return tuple(((a, 0, start), (a, 1, start)) for a in shards)

    def event_0():
        q_copy(2).wait_recv()

    def event_1():
        q_copy(0).wait_recv()
        q_copy(4).start()
        next_stretch(1)
        arrive(2)
        pass_on(2)
        q_copy(3).wait_recv()
        q_copy(5).start()
        q_copy(1).wait_recv()
        arrive(3)
        pass_on(3)

    def event_4():
        next_stretch(2)
        pass_on(4, 5)
        q_copy(4).wait_recv()
        q_copy(5).wait_recv()

    def turns(table, count, events):
        def tile(n, u):
            found = [jnp.int32(value) for value in table[0][u]]
            for when in range(1, len(table)):
                found = [jnp.where(n == when, value, old) for value, old in zip(table[when][u], found)]
            return found

        def one_turn(n, carry):
            for when, event in events.items():
                pl.when(n == when)(event)
            one, two, after = tile(n, 0), tile(n, 1), tile(n + 1, 0)
            score(*two, count, 1)
            weigh(*one, count, 0)
            score(*after, count, 0)
            weigh(*two, count, 1)
            return carry

        score(*table[0][0], count, 0)
        lax.fori_loop(0, len(table) - 1, one_turn, 0)
        one, two = table[-1]
        score(*two, count, 1)
        weigh(*one, count, 0)
        weigh(*two, count, 1)

    arrive(0, 1)
    pass_on(0, 1)
    loads[OWN + 1].wait()
    turns(first_turns, 8, {0: event_0, 1: event_1})
    turns(whole(8, 0), 4, {})
    arrive(4, 5)
    turns(more_turns, 8, {1: event_4})
    arrive(6, 7)

    def event_third():
        next_stretch(3)
        pass_on(6, 7)

    turns(whole(16, 3, 1, 2), 4, {1: event_third})
    arrive(8, 9)
    pass_on(8, 9)
    turns(whole(20, 3, 1, 2), 4, {})

    def stretch(a, row):
        pairs = [(j - y + NY) % NY for j in range(row + 1)]
        keys = jnp.concatenate([st[pl.ds(2 * k, 2), pl.ds(0, TOK), :].reshape(2 * TOK, HD) for k in pairs], axis=0)
        vals = jnp.concatenate([st[2 * k + n, pl.ds(TOK, HD), :] for k in pairs for n in (0, 1)], axis=1)
        vals = jnp.concatenate([vals, jnp.ones((SUMS, 2 * TOK * (row + 1)), jnp.bfloat16)], axis=0)
        key = lax.broadcasted_iota(jnp.int32, (2 * TOK, TILE), 0)
        token = lax.broadcasted_iota(jnp.int32, (2 * TOK, TILE), 1) // GROUP
        key_pos = pairs[row] * TOK + key + jnp.where(key >= TOK, NY * TOK - TOK, 0)
        scored = []
        for half in (0, 1):
            s = lax.dot_general(keys, qs[columns(a, half), :], NT, preferred_element_type=jnp.float32)
            usable = key_pos <= z * TOK + half * (TILE // GROUP) + token
            own = jnp.where(usable, s[row * 2 * TOK:, :], LOWEST)
            scored.append(own if row == 0 else jnp.concatenate([s[:row * 2 * TOK, :], own], axis=0))
        for half in (0, 1):
            add(columns(a, half), scored[half], vals)

    def stretch_of(a):
        offset = jnp.where(a == 3, 2, jnp.where(a == 2, 3, a))
        mine_row = (y + offset) % NY
        for row in range(NY):
            pl.when(mine_row == row)(functools.partial(stretch, a, row))

    next_stretch(4)

    def third_step():
        arrive(10, 11)
        turns(whole(24, 3), 4, {})

    def stretch_turn(n, carry):
        pl.when(n == 1)(third_step)
        stretch_of(jnp.where(n == 0, 3, 1))
        return carry

    lax.fori_loop(0, 2, stretch_turn, 0)

    def finish(a, half):
        cols = columns(a, half)
        part = acc[:, cols]
        total = part[HD:HD + 1, :]
        return part[:HD, :] * (1.0 / total), top[:, cols] + jnp.log2(total)

    def join(parts):
        peak = functools.reduce(jnp.maximum, [level for _, level in parts])
        shares = [jnp.exp2(level - peak) for _, level in parts]
        total = functools.reduce(jnp.add, shares)
        result = functools.reduce(
            jnp.add, [part.astype(jnp.float32) * (share / total) for (part, _), share in zip(parts, shares)]
        )
        return result, peak + jnp.log2(total)

    def arrived(n):
        for copy in o_copies(n):
            copy.wait_recv()
        return oget[n], lget[n]

    def send(n, result, level):
        osend[n] = result.astype(jnp.bfloat16)
        lsend[n] = level
        for copy in o_copies(n):
            copy.start()

    arrive(12, 13)
    turns(whole(28, 3), 4, {})
    for half in (0, 1):
        send(half, *finish(3, half))
    stretch_of(2)
    order = ((1, 1), (2, 0), (1, 0), (2, 1))
    score(*order[0], 24, 8, 0)
    for n, (a, half) in enumerate(order):
        if n + 1 < len(order):
            score(*order[n + 1], 24, 8, (n + 1) % 2)
        weigh(a, half, 24, 8, n % 2)
        if n == 1:
            send(3, *finish(1, 1))
            send(4, *finish(2, 0))
    send(2, *join([finish(1, 0), arrived(0)]))
    send(5, *join([finish(2, 1), arrived(1)]))
    turns(whole(12, 0), 4, {})
    turns(whole(16, 0) + whole(24, 0), 8, {})
    stretch_of(0)

    for d in range(1, HEADS):
        page_copy(d, (me - d + HEADS) % HEADS).wait_recv()
    own_pages().wait()
    for h in range(HEADS):
        paged[pl.ds(h, 4 * BLOCK, stride=HEADS), :] = landed[h].astype(jnp.float32)
    moved[...] = paged[pl.ds(0, 4 * BLOCK * HEADS), :].astype(jnp.bfloat16)

    levels = []
    for half in (0, 1):
        result, level = join([finish(0, half), arrived((4, 3)[half])])
        acc[pl.ds(0, HD), columns(0, half)] = result
        levels.append(level)
    for half in (0, 1):
        result, _ = join([(acc[pl.ds(0, HD), columns(0, half)], levels[half]), arrived((2, 5)[half])])
        out[pl.ds(half * TILE, TILE), :] = result.T.astype(jnp.bfloat16)

    for m in range(MSGS):
        for forward in (True, False):
            kv_copy(m, forward).wait_send()
    for n in range(6):
        q_copy(n).wait_send()
    for hop in (1, 2, 3, 4):
        for forward in (True, False):
            st_copy(hop, forward, True).wait_send()

    @pl.when(z % NY != 0)
    def _():
        shift_copy().wait_send()

    for n in range(6):
        for copy in o_copies(n):
            copy.wait_send()
    for d in range(1, HEADS):
        page_copy(d, me).wait_send()


def write(out_in, moved_in, out, moved, sems):
    copies = [
        pltpu.make_async_copy(out_in.at[pl.ds(n * 256, 256)], out.at[pl.ds(n * 256, 256)], sems.at[n]) for n in range(4)
    ]
    copies += [
        pltpu.make_async_copy(moved_in.at[pl.ds(n * 256, 256)], moved.at[pl.ds(n * 256, 256)], sems.at[4 + n])
        for n in range(2)
    ]
    for copy in copies:
        copy.start()
    for copy in copies:
        copy.wait()


def body(queries, cache_kv, new_kv, cache_lengths, plan):
    smem = pl.BlockSpec(memory_space=pltpu.SMEM)
    hbm = pl.BlockSpec(memory_space=pltpu.HBM)
    out, moved = pl.pallas_call(
        kernel,
        out_shape=(
            jax.ShapeDtypeStruct((ROWS, HD), jnp.bfloat16),
            jax.ShapeDtypeStruct((4 * BLOCK * HEADS, HD), jnp.bfloat16),
        ),
        in_specs=[smem, smem, hbm, hbm, hbm],
        out_specs=(pl.BlockSpec(memory_space=pltpu.VMEM),) * 2,
        scratch_shapes=[
            pltpu.VMEM((PIECES, PIECE + HD, HD), jnp.bfloat16),
            pltpu.VMEM((NZ + 1, TOK + HD, HD), jnp.bfloat16),
            pltpu.VMEM((SUMS, PIECES * PIECE), jnp.bfloat16),
            pltpu.VMEM((NY * ROWS, HD), jnp.bfloat16),
            pltpu.VMEM((HD + SUMS, NY * ROWS), jnp.float32),
            pltpu.VMEM((1, NY * ROWS), jnp.float32),
            pltpu.VMEM((2, MOST * PIECE, TILE), jnp.float32),
            pltpu.VMEM((OWN, 2 * PIECE, HD), jnp.bfloat16),
            pltpu.VMEM((2 * TOK, HD), jnp.bfloat16),
            pltpu.VMEM((OWN + 1, 2 * PIECE + 8, HD), jnp.float32),
            pltpu.VMEM((HEADS, 4 * BLOCK, HD), jnp.bfloat16),
            pltpu.VMEM((HEADS, 4 * BLOCK, HD), jnp.bfloat16),
            pltpu.VMEM((4 * BLOCK * HEADS + 8, HD), jnp.float32),
            pltpu.VMEM((6, HD, TILE), jnp.bfloat16),
            pltpu.VMEM((6, 1, TILE), jnp.float32),
            pltpu.VMEM((6, HD, TILE), jnp.bfloat16),
            pltpu.VMEM((6, 1, TILE), jnp.float32),
            pltpu.SemaphoreType.DMA((OWN + 2,)),
            pltpu.SemaphoreType.DMA((PIECES,)),
            pltpu.SemaphoreType.DMA((PIECES,)),
            pltpu.SemaphoreType.DMA((4, 2)),
            pltpu.SemaphoreType.DMA((4, 2)),
            pltpu.SemaphoreType.DMA,
            pltpu.SemaphoreType.DMA,
            pltpu.SemaphoreType.DMA((6,)),
            pltpu.SemaphoreType.DMA((6,)),
            pltpu.SemaphoreType.DMA((6,)),
            pltpu.SemaphoreType.DMA((6,)),
            pltpu.SemaphoreType.DMA((6,)),
            pltpu.SemaphoreType.DMA((6,)),
            pltpu.SemaphoreType.DMA((HEADS,)),
            pltpu.SemaphoreType.DMA((HEADS,)),
            pltpu.SemaphoreType.DMA,
        ],
        compiler_params=pltpu.CompilerParams(
            collective_id=0, has_side_effects=True, vmem_limit_bytes=32 * 2 ** 20
        ),
        name="stretch_attention",
    )(
        *(pltpu.with_memory_space_constraint(x, pltpu.HBM) for x in (
            cache_lengths,
            plan.reshape(PAGES),
            queries.reshape(ROWS, HD),
            cache_kv.reshape(2 * CACHE, HD),
            new_kv.reshape(2 * TOK, HD),
        )),
    )
    vmem = pl.BlockSpec(memory_space=pltpu.VMEM)
    out, moved = pl.pallas_call(
        write,
        out_shape=(
            jax.ShapeDtypeStruct((ROWS, HD), jnp.bfloat16),
            jax.ShapeDtypeStruct((4 * BLOCK * HEADS, HD), jnp.bfloat16),
        ),
        in_specs=[vmem, vmem],
        out_specs=(hbm, hbm),
        scratch_shapes=[pltpu.SemaphoreType.DMA((6,))],
        name="write_results",
    )(*(pltpu.with_memory_space_constraint(x, pltpu.VMEM) for x in (out, moved)))
    attended = out.reshape(TOK, 1, GROUP, HD)
    migrated = moved.reshape(1, 1, 2, BLOCK, 2, HEADS, HD)
    return attended, migrated


def solution(mesh):
    return jax.shard_map(
        body,
        mesh=mesh,
        in_specs=(
            P("ctx", ("head", "inst"), None, None),
            P("ctx", None, ("head", "inst"), None),
            P("ctx", None, ("head", "inst"), None),
            P(),
            P("ctx", None),
        ),
        out_specs=(
            P("ctx", ("head", "inst"), None, None),
            P("inst", "ctx", "head", None, None, None, None),
        ),
        check_vma=False,
    )
```
